512 devices in a mesh: dp: 64 (over x, z, y_hi), layer: 8 (over y_lo, core).
Axes of the slice: x: 4, y: 8 (y_hi: 2, y_lo: 4; y = y_hi * 4 + y_lo), z: 8, core: 2. Of those that a mesh axis runs over, the one named last changes fastest.
Arguments:
- grad: bfloat16 [16384, 2048], P(('layer', 'dp')), parts along dimension 0, may hold values from -0.59765625 to 0.59765625
- left_gram: float32 [16384, 2048], P(('layer', 'dp')), parts along dimension 0, may hold values from -0.2 to 17
- basis: float32 [16384, 512], P(('layer', 'dp')), parts along dimension 0, may hold values from -6 to 6
- exp_avg: float32 [16384, 512], P(('layer', 'dp')), parts along dimension 0, may hold values from -6 to 6
- exp_avg_sq: float32 [16384, 512], P(('layer', 'dp')), parts along dimension 0, may hold values from 0.01 to 1
Outputs:
- left_gram_new: float32 [16384, 2048], P(('layer', 'dp')), parts along dimension 0
- basis_new: float32 [16384, 512], P(('layer', 'dp')), parts along dimension 0
- exp_avg_new: float32 [16384, 512], P(('layer', 'dp')), parts along dimension 0
- exp_avg_sq_new: float32 [16384, 512], P(('layer', 'dp')), parts along dimension 0
The draws below stay inside these ranges and needn't reach their ends.
There are 8 independent parts, one for each index of `layer`. The reference program is written for one: setup_inputs(seed, part) draws one part's arguments, and reference() takes and returns one part's arrays. A program takes and returns all parts, laid end to end along the dimension named above; each array names one. Nothing has to cross between parts.
All inputs are finite; a program needn't handle non-finite values.
Results may differ from the reference program's by a relative error of at most 0.003.
The reference program's roundings to bfloat16 on the way (of `wire_basis`) count: a program that leaves them out, or rounds other values in their place, can miss the bound.
Values may be sent and summed in bfloat16 or wider, within the bound.
A program may use at most 64 MiB of HBM per device.

```python
import math
import jax
import jax.numpy as jnp
from jax import lax

D = 2048
E = 2048
K = 512


def draw_left_gram(key, part):
    key_off = jax.random.fold_in(key, 11)
    key_diag = jax.random.fold_in(key, 12)
    key_sign = jax.random.fold_in(key, 13)
    key_size = jax.random.fold_in(key, 14)
    signs = jnp.where(jax.random.bernoulli(key_sign, 0.5, (D,)), 1.0, -1.0).astype(jnp.float32)
    shared = signs * jax.random.uniform(key_size, (D,), jnp.float32, 0.5, 1.5)
    raw = jnp.clip(jax.random.normal(key_off, (D, D), jnp.float32), -6.0, 6.0)
    diag = jnp.exp(jax.random.uniform(key_diag, (D,), jnp.float32, 0.0, jnp.log(10.0)))
    common = 0.01
    off = 0.5 * (raw + raw.T) * 0.009
    return off + common * (shared[:, None] * shared[None, :]) + jnp.diag(diag)


def shard_levels(own_key, dims, split, least, largest):
    loudness, own = 1.0, jax.random.fold_in(own_key, 6)
    for position, shards_of in split:
        draws = jnp.exp(jax.random.uniform(jax.random.fold_in(own, position), (shards_of,), jnp.float32, least / len(split), largest / len(split)))
        loudness = loudness * jnp.repeat(draws, dims[position] // shards_of).reshape([-1 if axis == position else 1 for axis in range(len(dims))])
    return loudness


def normal_values(key, extent, width, reach, shards=(), held_as=jnp.bfloat16):
    level = shard_levels(key, extent, shards, -0.22, 0.18) if shards else 1.0
    drawn = jax.random.normal(key, extent, jnp.float32) * width * level
    return jnp.minimum(jnp.maximum(drawn, -reach), reach).astype(held_as)


def setup_inputs(seed: int = 0, part: int = 0) -> dict:
    splits = jax.random.split(jax.random.key(seed), 6)
    part_splits = jax.random.split(jax.random.fold_in(splits[5], part), 6)
    grad = normal_values(part_splits[0], (D, E), 0.1, 0.59765625, ((0, 64),))
    left_gram = draw_left_gram(jax.random.fold_in(jax.random.fold_in(splits[5], part), 71), part)
    basis = normal_values(part_splits[2], (D, K), 1.0, 6.0, ((0, 64),), jnp.float32)
    exp_avg = normal_values(part_splits[3], (E, K), 1.0, 6.0, ((0, 64),), jnp.float32)
    exp_avg_sq = jnp.clip(jnp.exp(math.log(1.0) - 4.6051702 * jax.random.uniform(part_splits[4], (E, K), jnp.float32) ** shard_levels(part_splits[4], (E, K), ((0, 64),), -0.2, 0.2)), 0.01, 1.0)
    return {"grad": grad, "left_gram": left_gram, "basis": basis, "exp_avg": exp_avg, "exp_avg_sq": exp_avg_sq}


def lower_solve(lower, right):
    return lax.linalg.triangular_solve(lower, right, left_side=True, lower=True)

def reference(grad, left_gram, basis, exp_avg, exp_avg_sq):
    gram = jnp.dot(grad.astype(jnp.float32), grad.T.astype(jnp.float32), preferred_element_type=jnp.float32)
    left_gram_new = 0.95 * left_gram + 0.05 * gram
    wire_basis = lax.optimization_barrier(basis.astype(jnp.bfloat16)).astype(jnp.float32)
    power = jnp.dot(left_gram_new, wire_basis, precision=lax.Precision.HIGHEST)
    first_gram = jnp.dot(power.T, power, precision=lax.Precision.HIGHEST)
    cross = jnp.dot(power.T, wire_basis, precision=lax.Precision.HIGHEST)
    lower_one = jnp.linalg.cholesky(first_gram)
    scale = math.sqrt(D)
    basis_new = scale * lower_solve(lower_one, power.T).T
    rotation = lower_solve(lower_one, cross) / scale
    exp_avg_new = jnp.dot(exp_avg, rotation.T, precision=lax.Precision.HIGHEST)
    exp_avg_sq_new = jnp.dot(exp_avg_sq, (rotation * rotation).T, precision=lax.Precision.HIGHEST)
    return (left_gram_new, basis_new, exp_avg_new, exp_avg_sq_new)
```

```python
import functools
import math

import jax
import jax.numpy as jnp
from jax import lax
from jax.experimental import pallas as pl
from jax.experimental.pallas import tpu as pltpu
from jax.sharding import PartitionSpec as P

D = 2048
K = 512
R = 32
HIGHEST = lax.Precision.HIGHEST
F32 = jnp.float32
BF16 = jnp.bfloat16
GA, GB, WA, WB, LG, GN, PP, PG, FR, CR, FA, CA, FB, CB = range(14)


def dot(a, b, dims, precision=None):
    return lax.dot_general(a, b, (dims, ((), ())), precision=precision, preferred_element_type=F32)


def split_columns(lg_ref, out_ref):
    low = lax.broadcasted_iota(jnp.int32, (R, 128), 1) < 64
    for x in range(4):
        t = [lg_ref[:, x * 512 + k * 128 : x * 512 + (k + 1) * 128] for k in range(4)]
        for h in range(2):
            a, b = t[2 * h], t[2 * h + 1]
            out_ref[2 * x, :, h * 128 : (h + 1) * 128] = jnp.where(low, a, pltpu.roll(b, 64, 1))
            out_ref[2 * x + 1, :, h * 128 : (h + 1) * 128] = jnp.where(low, pltpu.roll(a, 64, 1), b)


def join_columns(in_ref, out_ref):
    low = lax.broadcasted_iota(jnp.int32, (R, 128), 1) < 64
    for x in range(4):
        for h in range(2):
            a = in_ref[2 * x, :, h * 128 : (h + 1) * 128]
            b = in_ref[2 * x + 1, :, h * 128 : (h + 1) * 128]
            at = x * 512 + h * 256
            out_ref[:, at : at + 128] = jnp.where(low, a, pltpu.roll(b, 64, 1))
            out_ref[:, at + 128 : at + 256] = jnp.where(low, pltpu.roll(a, 64, 1), b)


def kernel(
    grad_ref, lg_ref, basis_ref,
    lgn_ref, pown_ref, f_ref, c_ref,
    ga, gb, wa, wb, lgs, lgr, gn, gback, pp, pr, pb, pt, fp, fr, cp, cr, fall, call,
    send_sem, recv_sem,
):
    me = lax.axis_index("dp")
    x, z21, z0, yh = me // 16, (me // 4) % 4, (me // 2) % 2, me % 2
    p = x * 2 + z0
    q = z21 * 2 + yh

    def device(pp_, qq_):
        return {"dp": (pp_ // 2) * 16 + (qq_ // 2) * 4 + (pp_ % 2) * 2 + qq_ % 2}

    def p_peers():
        return [(p + d) % 8 for d in range(1, 8)]

    def q_peers():
        return [(q + d) % 8 for d in range(1, 8)]

    barrier = pltpu.get_barrier_semaphore()
    for o in p_peers():
        pl.semaphore_signal(barrier, inc=1, device_id=device(o, q), device_id_type=pl.DeviceIdType.MESH)
    for o in q_peers():
        pl.semaphore_signal(barrier, inc=1, device_id=device(p, o), device_id_type=pl.DeviceIdType.MESH)

    def rows(ref, i, n=R):
        return ref.at[pl.ds(pl.multiple_of(i * n, n), n)]

    def copy(phase, src, dst, to, slot_from, dev):
        return pltpu.make_async_remote_copy(
            src_ref=src, dst_ref=dst,
            send_sem=send_sem.at[phase, to], recv_sem=recv_sem.at[phase, slot_from],
            device_id=dev, device_id_type=pl.DeviceIdType.MESH,
        )

    started = []

    def send_p(phase, src, dst):
        for o in p_peers():
            c = copy(phase, src(o), dst(p), o, p, device(o, q))
            c.start()
            started.append(c)

    def send_q(phase, src, dst):
        for o in q_peers():
            c = copy(phase, src(o), dst(q), o, q, device(p, o))
            c.start()
            started.append(c)

    def wait_p(phase, dst):
        for o in p_peers():
            copy(phase, dst(o), dst(o), o, o, device(o, q)).wait_recv()

    def wait_q(phase, dst):
        for o in q_peers():
            copy(phase, dst(o), dst(o), o, o, device(p, o)).wait_recv()

    rows(wa, q)[...] = basis_ref[...].astype(BF16)
    rows(wb, p)[...] = basis_ref[...].astype(BF16)
    pl.semaphore_wait(barrier, 14)
    send_p(GB, lambda o: grad_ref, lambda i: rows(gb, i))
    send_q(GA, lambda o: grad_ref, lambda i: rows(ga, i))
    split_columns(lg_ref, lgs)
    send_p(LG, lambda o: lgs.at[o], lambda i: lgr.at[i])
    send_q(WA, lambda o: rows(wa, q), lambda i: rows(wa, i))
    send_p(WB, lambda o: rows(wb, p), lambda i: rows(wb, i))
    rows(ga, q)[...] = grad_ref[...]
    rows(gb, p)[...] = grad_ref[...]
    lgr[p] = lgs[p]
    wait_p(GB, lambda i: rows(gb, i))
    wait_q(GA, lambda i: rows(ga, i))
    wait_p(LG, lambda i: lgr.at[i])
    gram = dot(gb[...], ga[...], ((1,), (1,)))
    new = 0.95 * lgr[...].reshape(256, 256) + 0.05 * gram
    gn[...] = new.reshape(8, R, 256)
    gback[p] = gn[p]
    wait_q(WA, lambda i: rows(wa, i))
    high = new.astype(BF16)
    rest = new - high.astype(F32)
    mid = rest.astype(BF16)
    low = (rest - mid.astype(F32)).astype(BF16)
    w = wa[...]
    part = dot(high, w, ((1,), (0,))) + (dot(mid, w, ((1,), (0,))) + dot(low, w, ((1,), (0,))))
    pp[...] = part.reshape(8, R, K)
    send_p(PP, lambda o: pp.at[o], lambda i: pr.at[i])
    pr[p] = pp[p]
    wait_p(PP, lambda i: pr.at[i])
    own = pr[0]
    for i in range(1, 8):
        own = own + pr[i]
    pown_ref[...] = own
    rows(pb, p)[...] = own
    send_p(PG, lambda o: rows(pb, p), lambda i: rows(pb, i))
    send_p(GN, lambda o: gn.at[o], lambda i: gback.at[i])
    wait_p(WB, lambda i: rows(wb, i))
    wait_p(PG, lambda i: rows(pb, i))
    pt[...] = pb[...].T
    left = rows(pt, p, 64)[...]
    fp[...] = dot(left, pb[...], ((1,), (0,)), HIGHEST).reshape(8, 8, K)
    send_q(FR, lambda o: fp.at[o], lambda i: fr.at[i])
    cp[...] = dot(left, wb[...].astype(F32), ((1,), (0,)), HIGHEST).reshape(8, 8, K)
    send_q(CR, lambda o: cp.at[o], lambda i: cr.at[i])
    fr[q] = fp[q]
    cr[q] = cp[q]

    def total(ref):
        s = ref[0]
        for i in range(1, 8):
            s = s + ref[i]
        return s

    wait_q(FR, lambda i: fr.at[i])
    fall[p * 8 + q] = total(fr)
    send_q(FA, lambda o: fall.at[p * 8 + q], lambda i: fall.at[p * 8 + i])
    wait_q(CR, lambda i: cr.at[i])
    call[p * 8 + q] = total(cr)
    send_q(CA, lambda o: call.at[p * 8 + q], lambda i: call.at[p * 8 + i])
    wait_q(FA, lambda i: fall.at[p * 8 + i])
    send_p(FB, lambda o: rows(fall, p, 8), lambda i: rows(fall, i, 8))
    wait_q(CA, lambda i: call.at[p * 8 + i])
    send_p(CB, lambda o: rows(call, p, 8), lambda i: rows(call, i, 8))
    wait_p(GN, lambda i: gback.at[i])
    join_columns(gback, lgn_ref)
    wait_p(FB, lambda i: rows(fall, i, 8))
    f_ref[...] = fall[...].reshape(K, K)
    wait_p(CB, lambda i: rows(call, i, 8))
    c_ref[...] = call[...].reshape(K, K)
    for c in started:
        c.wait_send()


def lower_solve(lower, right):
    return lax.linalg.triangular_solve(lower, right, left_side=True, lower=True)


def body(grad, left_gram, basis, exp_avg, exp_avg_sq):
    vm = pl.BlockSpec(memory_space=pltpu.VMEM)
    sds = jax.ShapeDtypeStruct
    left_gram_new, power, first_gram, cross = pl.pallas_call(
        kernel,
        out_shape=(sds((R, D), F32), sds((R, K), F32), sds((K, K), F32), sds((K, K), F32)),
        in_specs=[vm] * 3,
        out_specs=(vm,) * 4,
        scratch_shapes=[
            pltpu.VMEM((256, D), BF16), pltpu.VMEM((256, D), BF16),
            pltpu.VMEM((256, K), BF16), pltpu.VMEM((256, K), BF16),
            pltpu.VMEM((8, R, 256), F32), pltpu.VMEM((8, R, 256), F32),
            pltpu.VMEM((8, R, 256), F32), pltpu.VMEM((8, R, 256), F32),
            pltpu.VMEM((8, R, K), F32), pltpu.VMEM((8, R, K), F32),
            pltpu.VMEM((256, K), F32), pltpu.VMEM((K, 256), F32),
            pltpu.VMEM((8, 8, K), F32), pltpu.VMEM((8, 8, K), F32),
            pltpu.VMEM((8, 8, K), F32), pltpu.VMEM((8, 8, K), F32),
            pltpu.VMEM((64, 8, K), F32), pltpu.VMEM((64, 8, K), F32),
            pltpu.SemaphoreType.DMA((14, 8)), pltpu.SemaphoreType.DMA((14, 8)),
        ],
        compiler_params=pltpu.CompilerParams(
            collective_id=0, has_side_effects=True, vmem_limit_bytes=48 * 1024 * 1024
        ),
        cost_estimate=pl.CostEstimate(flops=500_000_000, bytes_accessed=4_000_000, transcendentals=0),
        name="gram_power",
    )(grad, left_gram, basis)
    scale = math.sqrt(D)
    lower_one = jnp.linalg.cholesky(first_gram)
    both = lower_solve(lower_one, jnp.concatenate([power.T, cross], axis=1))
    basis_new = scale * both[:, :R].T
    rotation = both[:, R:] / scale
    exp_avg_new = jnp.dot(exp_avg, rotation.T, precision=HIGHEST)
    exp_avg_sq_new = jnp.dot(exp_avg_sq, (rotation * rotation).T, precision=HIGHEST)
    return (left_gram_new, basis_new, exp_avg_new, exp_avg_sq_new)


def solution(mesh):
    placed = P(("layer", "dp"), None)
    return jax.shard_map(
        body, mesh=mesh, in_specs=(placed,) * 5, out_specs=(placed,) * 4, check_vma=False
    )
```

```python
import functools
import math

import jax
import jax.numpy as jnp
from jax import lax
from jax.experimental import pallas as pl
from jax.experimental.pallas import tpu as pltpu
from jax.sharding import PartitionSpec as P

D = 2048
K = 512
R = 32
HIGHEST = lax.Precision.HIGHEST
F32 = jnp.float32
BF16 = jnp.bfloat16
GA, GB, WA, WB, LG, GN, PP, PG, FR, CR, FA, CA, FB, CB = range(14)


def dot(a, b, dims, precision=None):
    return lax.dot_general(a, b, (dims, ((), ())), precision=precision, preferred_element_type=F32)


def dot3(a, b, dims):
    ah, bh = a.astype(BF16), b.astype(BF16)
    al, bl = (a - ah.astype(F32)).astype(BF16), (b - bh.astype(F32)).astype(BF16)
    return dot(ah, bh, dims) + (dot(ah, bl, dims) + dot(al, bh, dims))


def lane(v, k):
    return jnp.broadcast_to(v[:, k : k + 1], (8, 128))


def sub(v, t):
    return jnp.broadcast_to(v[t : t + 1, :], (8, 128))


def inverse_factor(a_rows):
    row = lax.broadcasted_iota(jnp.int32, (8, 128), 0)
    col = lax.broadcasted_iota(jnp.int32, (8, 128), 1)
    n = len(a_rows)
    a_rows = list(a_rows)
    e_rows = [jnp.where(col == row + 8 * i, 1.0, 0.0).astype(F32) for i in range(n)]
    out = []
    for m in range(n):
        r_m, s_m = a_rows[m], e_rows[m]
        c = [lane(r_m, 8 * m + t) for t in range(8)]
        v = jnp.zeros((8, 128), F32)
        for t in range(8):
            here = row == t
            pivot = sub(c[t], t)
            inv = 1.0 / pivot
            s_t = sub(s_m, t)
            v = jnp.where(here, s_t * lax.rsqrt(pivot), v)
            mult = jnp.where(here, -1.0, c[t])
            for u in range(t + 1, 8):
                c[u] = jnp.where(here, 0.0, c[u]) - mult * (sub(c[u], t) * inv)
            if m < n - 1:
                r_m = jnp.where(here, 0.0, r_m) - mult * (sub(r_m, t) * inv)
                s_m = jnp.where(here, 0.0, s_m) - mult * (s_t * inv)
            elif t < 7:
                s_m = jnp.where(here, 0.0, s_m) - mult * (s_t * inv)
        out.append(v)
        if m < n - 1:
            w = [sub(r_m, t) for t in range(8)]
            s = [sub(s_m, t) for t in range(8)]
            for i in range(m + 1, n):
                l = [lane(a_rows[i], 8 * m + t) for t in range(8)]
                for t in range(8):
                    a_rows[i] = a_rows[i] - l[t] * w[t]
                    e_rows[i] = e_rows[i] - l[t] * s[t]
    return out


def split_columns(lg_ref, out_ref):
    low = lax.broadcasted_iota(jnp.int32, (R, 128), 1) < 64
    for x in range(4):
        t = [lg_ref[:, x * 512 + k * 128 : x * 512 + (k + 1) * 128] for k in range(4)]
        for h in range(2):
            a, b = t[2 * h], t[2 * h + 1]
            out_ref[2 * x, :, h * 128 : (h + 1) * 128] = jnp.where(low, a, pltpu.roll(b, 64, 1))
            out_ref[2 * x + 1, :, h * 128 : (h + 1) * 128] = jnp.where(low, pltpu.roll(a, 64, 1), b)


def join_columns(in_ref, out_ref):
    low = lax.broadcasted_iota(jnp.int32, (R, 128), 1) < 64
    for x in range(4):
        for h in range(2):
            a = in_ref[2 * x, :, h * 128 : (h + 1) * 128]
            b = in_ref[2 * x + 1, :, h * 128 : (h + 1) * 128]
            at = x * 512 + h * 256
            out_ref[:, at : at + 128] = jnp.where(low, a, pltpu.roll(b, 64, 1))
            out_ref[:, at + 128 : at + 256] = jnp.where(low, pltpu.roll(a, 64, 1), b)


def kernel(
    grad_ref, lg_ref, basis_ref, avg_ref, sq_ref,
    lgn_ref, basis_out, avg_out, sq_out,
    ga, gb, wa, wb, lgs, lgr, gn, gback, pp, pr, pb, pt, fp, fr, cp, cr, fall, call, yf, yc, diag, inverse,
    send_sem, recv_sem,
):
    me = lax.axis_index("dp")
    x, z21, z0, yh = me // 16, (me // 4) % 4, (me // 2) % 2, me % 2
    p = x * 2 + z0
    q = z21 * 2 + yh

    def device(pp_, qq_):
        return {"dp": (pp_ // 2) * 16 + (qq_ // 2) * 4 + (pp_ % 2) * 2 + qq_ % 2}

    def p_peers():
        return [(p + d) % 8 for d in range(1, 8)]

    def q_peers():
        return [(q + d) % 8 for d in range(1, 8)]

    barrier = pltpu.get_barrier_semaphore()
    for o in p_peers():
        pl.semaphore_signal(barrier, inc=1, device_id=device(o, q), device_id_type=pl.DeviceIdType.MESH)
    for o in q_peers():
        pl.semaphore_signal(barrier, inc=1, device_id=device(p, o), device_id_type=pl.DeviceIdType.MESH)

    def rows(ref, i, n=R):
        return ref.at[pl.ds(pl.multiple_of(i * n, n), n)]

    def copy(phase, src, dst, to, slot_from, dev):
        return pltpu.make_async_remote_copy(
            src_ref=src, dst_ref=dst,
            send_sem=send_sem.at[phase, to], recv_sem=recv_sem.at[phase, slot_from],
            device_id=dev, device_id_type=pl.DeviceIdType.MESH,
        )

    started = []

    def send_p(phase, src, dst):
        for o in p_peers():
            c = copy(phase, src(o), dst(p), o, p, device(o, q))
            c.start()
            started.append(c)

    def send_q(phase, src, dst):
        for o in q_peers():
            c = copy(phase, src(o), dst(q), o, q, device(p, o))
            c.start()
            started.append(c)

    def wait_p(phase, dst):
        for o in p_peers():
            copy(phase, dst(o), dst(o), o, o, device(o, q)).wait_recv()

    def wait_q(phase, dst):
        for o in q_peers():
            copy(phase, dst(o), dst(o), o, o, device(p, o)).wait_recv()

    rows(wa, q)[...] = basis_ref[...].astype(BF16)
    rows(wb, p)[...] = basis_ref[...].astype(BF16)
    pl.semaphore_wait(barrier, 14)
    send_p(GB, lambda o: grad_ref, lambda i: rows(gb, i))
    send_q(GA, lambda o: grad_ref, lambda i: rows(ga, i))
    split_columns(lg_ref, lgs)
    send_p(LG, lambda o: lgs.at[o], lambda i: lgr.at[i])
    send_q(WA, lambda o: rows(wa, q), lambda i: rows(wa, i))
    send_p(WB, lambda o: rows(wb, p), lambda i: rows(wb, i))
    rows(ga, q)[...] = grad_ref[...]
    rows(gb, p)[...] = grad_ref[...]
    lgr[p] = lgs[p]
    wait_p(GB, lambda i: rows(gb, i))
    wait_q(GA, lambda i: rows(ga, i))
    wait_p(LG, lambda i: lgr.at[i])
    gram = dot(gb[...], ga[...], ((1,), (1,)))
    new = 0.95 * lgr[...].reshape(256, 256) + 0.05 * gram
    gn[...] = new.reshape(8, R, 256)
    gback[p] = gn[p]
    wait_q(WA, lambda i: rows(wa, i))
    high = new.astype(BF16)
    rest = new - high.astype(F32)
    mid = rest.astype(BF16)
    low = (rest - mid.astype(F32)).astype(BF16)
    w = wa[...]
    part = dot(high, w, ((1,), (0,))) + (dot(mid, w, ((1,), (0,))) + dot(low, w, ((1,), (0,))))
    pp[...] = part.reshape(8, R, K)
    send_p(PP, lambda o: pp.at[o], lambda i: pr.at[i])
    pr[p] = pp[p]
    wait_p(PP, lambda i: pr.at[i])
    own = pr[0]
    for i in range(1, 8):
        own = own + pr[i]
    rows(pb, p)[...] = own
    send_p(PG, lambda o: rows(pb, p), lambda i: rows(pb, i))
    send_p(GN, lambda o: gn.at[o], lambda i: gback.at[i])
    yf[...] = jnp.zeros_like(yf)
    yc[...] = jnp.zeros_like(yc)
    call[:, K:] = jnp.zeros((K, 128), F32)
    call[:, K : K + R] = own.T
    wait_p(WB, lambda i: rows(wb, i))
    wait_p(PG, lambda i: rows(pb, i))
    pt[...] = pb[...].T
    left = rows(pt, p, 64)[...]
    fp[...] = dot(left, pb[...], ((1,), (0,)), HIGHEST).reshape(8, 8, K)
    send_q(FR, lambda o: fp.at[o], lambda i: fr.at[i])
    cp[...] = dot(left, wb[...].astype(F32), ((1,), (0,)), HIGHEST).reshape(8, 8, K)
    send_q(CR, lambda o: cp.at[o], lambda i: cr.at[i])
    fr[q] = fp[q]
    cr[q] = cp[q]

    def total(ref):
        s = ref[0]
        for i in range(1, 8):
            s = s + ref[i]
        return s

    def crow(i, n=8):
        return call.at[pl.ds(pl.multiple_of(i * n, n), n), pl.ds(0, K)]

    wait_q(FR, lambda i: fr.at[i])
    rows(fall, p * 8 + q, 8)[...] = total(fr)
    send_q(FA, lambda o: rows(fall, p * 8 + q, 8), lambda i: rows(fall, p * 8 + i, 8))
    wait_q(CR, lambda i: cr.at[i])
    crow(p * 8 + q)[...] = total(cr)
    send_q(CA, lambda o: crow(p * 8 + q), lambda i: crow(p * 8 + i))
    wait_q(FA, lambda i: rows(fall, p * 8 + i, 8))
    send_p(FB, lambda o: rows(fall, p, 64), lambda i: rows(fall, i, 64))
    wait_p(GN, lambda i: gback.at[i])
    join_columns(gback, lgn_ref)
    wait_q(CA, lambda i: crow(p * 8 + i))

    def wait_row(phase, ref, i):
        @pl.when(i != p)
        def _():
            copy(phase, ref(i), ref(i), i, i, device(i, q)).wait_recv()

    scale = math.sqrt(D)

    def block(k):
        return pl.ds(pl.multiple_of(k * 128, 128), 128)

    def main_rows(k):
        here = block(k)
        u = yf[:, here]
        a = fall[here, :] - dot(u, yf[...], ((0,), (0,)), HIGHEST)
        diag[...] = fall[here, here] - dot(u, u, ((0,), (0,)), HIGHEST)
        out = inverse_factor([diag[8 * i : 8 * i + 8, :] for i in range(16)])
        for i in range(16):
            inverse[k, 8 * i : 8 * i + 8, :] = out[i]
        yf[here, :] = dot(inverse[k], a, ((1,), (0,)), HIGHEST)

    def side_rows(k):
        here = block(k)
        a = call[here, :] - dot3(yf[:, here], yc[...], ((0,), (0,)))
        y = dot3(inverse[k], a, ((1,), (0,)))
        yc[here, :] = y
        basis_out[:, here] = (scale * y[:, K:]).T[:R, :]
        rotation = y[:, :K] / scale
        avg_out[:, here] = dot3(avg_ref[...], rotation, ((1,), (1,)))
        sq_out[:, here] = dot3(sq_ref[...], rotation * rotation, ((1,), (1,)))

    @pl.loop(0, 2)
    def _(k):
        wait_row(FB, lambda i: rows(fall, i, 64), 2 * k)
        wait_row(FB, lambda i: rows(fall, i, 64), 2 * k + 1)

        @pl.when(k == 0)
        def _():
            for o in p_peers():
                copy(CB, crow(p, 64), crow(p, 64), o, p, device(o, q)).start()

        main_rows(k)

    @pl.loop(2, 4)
    def _(k):
        for h in range(2):
            wait_row(FB, lambda i: rows(fall, i, 64), 2 * k + h)
            wait_row(CB, lambda i: crow(i, 64), 2 * (k - 2) + h)
        side_rows(k - 2)
        main_rows(k)

    for h in range(4, 8):
        wait_row(CB, lambda i: crow(i, 64), h)
    side_rows(2)
    side_rows(3)
    for o in p_peers():
        copy(CB, crow(p, 64), crow(p, 64), o, p, device(o, q)).wait_send()
    for c in started:
        c.wait_send()


def body(grad, left_gram, basis, exp_avg, exp_avg_sq):
    vm = pl.BlockSpec(memory_space=pltpu.VMEM)
    sds = jax.ShapeDtypeStruct
    return pl.pallas_call(
        kernel,
        out_shape=(sds((R, D), F32), sds((R, K), F32), sds((R, K), F32), sds((R, K), F32)),
        in_specs=[vm] * 5,
        out_specs=(vm,) * 4,
        scratch_shapes=[
            pltpu.VMEM((256, D), BF16), pltpu.VMEM((256, D), BF16),
            pltpu.VMEM((256, K), BF16), pltpu.VMEM((256, K), BF16),
            pltpu.VMEM((8, R, 256), F32), pltpu.VMEM((8, R, 256), F32),
            pltpu.VMEM((8, R, 256), F32), pltpu.VMEM((8, R, 256), F32),
            pltpu.VMEM((8, R, K), F32), pltpu.VMEM((8, R, K), F32),
            pltpu.VMEM((256, K), F32), pltpu.VMEM((K, 256), F32),
            pltpu.VMEM((8, 8, K), F32), pltpu.VMEM((8, 8, K), F32),
            pltpu.VMEM((8, 8, K), F32), pltpu.VMEM((8, 8, K), F32),
            pltpu.VMEM((K, K), F32), pltpu.VMEM((K, K + 128), F32),
            pltpu.VMEM((K, K), F32), pltpu.VMEM((K, K + 128), F32),
            pltpu.VMEM((128, 128), F32), pltpu.VMEM((4, 128, 128), F32),
            pltpu.SemaphoreType.DMA((14, 8)), pltpu.SemaphoreType.DMA((14, 8)),
        ],
        compiler_params=pltpu.CompilerParams(
            collective_id=0, has_side_effects=True, vmem_limit_bytes=48 * 1024 * 1024
        ),
        cost_estimate=pl.CostEstimate(flops=1_000_000_000, bytes_accessed=2_000_000, transcendentals=0),
        name="soap_refresh",
    )(grad, left_gram, basis, exp_avg, exp_avg_sq)


def solution(mesh):
    placed = P(("layer", "dp"), None)
    return jax.shard_map(
        body, mesh=mesh, in_specs=(placed,) * 5, out_specs=(placed,) * 4, check_vma=False
    )
```

```python
import functools
import math

import jax
import jax.numpy as jnp
from jax import lax
from jax.experimental import pallas as pl
from jax.experimental.pallas import tpu as pltpu
from jax.sharding import PartitionSpec as P

D = 2048
K = 512
R = 32
HIGHEST = lax.Precision.HIGHEST
F32 = jnp.float32
BF16 = jnp.bfloat16
LG, GN, PP, PG, FR, CR, FA, CA, FB, CB = range(10)
WIDE = D + K


def dot(a, b, dims, precision=None):
    return lax.dot_general(a, b, (dims, ((), ())), precision=precision, preferred_element_type=F32)


def dot3(a, b, dims):
    ah, bh = a.astype(BF16), b.astype(BF16)
    al, bl = (a - ah.astype(F32)).astype(BF16), (b - bh.astype(F32)).astype(BF16)
    return dot(ah, bh, dims) + (dot(ah, bl, dims) + dot(al, bh, dims))


def lane(v, k):
    return jnp.broadcast_to(v[:, k : k + 1], (8, 128))


def sub(v, t):
    return jnp.broadcast_to(v[t : t + 1, :], (8, 128))


def inverse_factor(a_rows, hooks={}):
    row = lax.broadcasted_iota(jnp.int32, (8, 128), 0)
    col = lax.broadcasted_iota(jnp.int32, (8, 128), 1)
    n = len(a_rows)
    a_rows = list(a_rows)
    e_rows = [jnp.where(col == row + 8 * i, 1.0, 0.0).astype(F32) for i in range(n)]
    out = []
    for m in range(n):
        hooks.get(m, lambda: None)()
        r_m, s_m = a_rows[m], e_rows[m]
        c = [lane(r_m, 8 * m + t) for t in range(8)]
        v = jnp.zeros((8, 128), F32)
        for t in range(8):
            here = row == t
            pivot = sub(c[t], t)
            inv = 1.0 / pivot
            s_t = sub(s_m, t)
            v = jnp.where(here, s_t * lax.rsqrt(pivot), v)
            mult = jnp.where(here, -1.0, c[t])
            for u in range(t + 1, 8):
                c[u] = jnp.where(here, 0.0, c[u]) - (mult * sub(c[u], t)) * inv
            if m < n - 1:
                r_m = jnp.where(here, 0.0, r_m) - (mult * sub(r_m, t)) * inv
                s_m = jnp.where(here, 0.0, s_m) - (mult * s_t) * inv
            elif t < 7:
                s_m = jnp.where(here, 0.0, s_m) - (mult * s_t) * inv
        out.append(v)
        if m < n - 1:
            w = [sub(r_m, t) for t in range(8)]
            s = [sub(s_m, t) for t in range(8)]
            for i in range(m + 1, n):
                l = [lane(a_rows[i], 8 * m + t) for t in range(8)]
                for t in range(8):
                    a_rows[i] = a_rows[i] - l[t] * w[t]
                    e_rows[i] = e_rows[i] - l[t] * s[t]
    return out


def split_columns(lg_ref, out_ref):
    low = lax.broadcasted_iota(jnp.int32, (R, 128), 1) < 64
    for x in range(4):
        t = [lg_ref[:, x * 512 + k * 128 : x * 512 + (k + 1) * 128] for k in range(4)]
        for h in range(2):
            a, b = t[2 * h], t[2 * h + 1]
            out_ref[2 * x, :, h * 128 : (h + 1) * 128] = jnp.where(low, a, pltpu.roll(b, 64, 1))
            out_ref[2 * x + 1, :, h * 128 : (h + 1) * 128] = jnp.where(low, pltpu.roll(a, 64, 1), b)


def join_columns(in_ref, out_ref):
    low = lax.broadcasted_iota(jnp.int32, (R, 128), 1) < 64
    for x in range(4):
        for h in range(2):
            a = in_ref[2 * x, :, h * 128 : (h + 1) * 128]
            b = in_ref[2 * x + 1, :, h * 128 : (h + 1) * 128]
            at = x * 512 + h * 256
            out_ref[:, at : at + 128] = jnp.where(low, a, pltpu.roll(b, 64, 1))
            out_ref[:, at + 128 : at + 256] = jnp.where(low, pltpu.roll(a, 64, 1), b)


def kernel(
    grad_hbm, lg_hbm, basis_hbm, avg_hbm, sq_hbm,
    lgn_ref, basis_out, avg_out, sq_out,
    lg_ref, basis_ref, avg_ref, sq_ref,
    ga, gb, lgs, lgr, gn, gback, pp, pr, pb, pt, fp, fr, cp, cr, fall, call, yf, yc, diag, inverse,
    send_sem, recv_sem, gather_send, gather_recv, in_sem,
):
    me = lax.axis_index("dp")
    x, z21, z0, yh = me // 16, (me // 4) % 4, (me // 2) % 2, me % 2
    p = x * 2 + z0
    q = z21 * 2 + yh

    def device(pp_, qq_):
        return {"dp": (pp_ // 2) * 16 + (qq_ // 2) * 4 + (pp_ % 2) * 2 + qq_ % 2}

    def p_peers():
        return [(p + d) % 8 for d in range(1, 8)]

    def q_peers():
        return [(q + d) % 8 for d in range(1, 8)]

    barrier = pltpu.get_barrier_semaphore()
    for o in p_peers():
        pl.semaphore_signal(barrier, inc=1, device_id=device(o, q), device_id_type=pl.DeviceIdType.MESH)
    for o in q_peers():
        pl.semaphore_signal(barrier, inc=1, device_id=device(p, o), device_id_type=pl.DeviceIdType.MESH)

    def rows(ref, i, n=R):
        return ref.at[pl.ds(pl.multiple_of(i * n, n), n)]

    def grad_rows(ref, i):
        return ref.at[pl.ds(pl.multiple_of(i * R, R), R), pl.ds(0, D)]

    def basis_rows(ref, i):
        return ref.at[pl.ds(pl.multiple_of(i * R, R), R), pl.ds(D, K)]

    loads = [
        pltpu.make_async_copy(basis_hbm, basis_ref, in_sem.at[0]),
        pltpu.make_async_copy(grad_hbm, grad_rows(ga, q), in_sem.at[1]),
        pltpu.make_async_copy(grad_hbm, grad_rows(gb, p), in_sem.at[2]),
        pltpu.make_async_copy(lg_hbm, lg_ref, in_sem.at[3]),
        pltpu.make_async_copy(avg_hbm, avg_ref, in_sem.at[4]),
        pltpu.make_async_copy(sq_hbm, sq_ref, in_sem.at[5]),
    ]
    for c in loads:
        c.start()

    def copy(phase, src, dst, to, slot_from, dev):
        return pltpu.make_async_remote_copy(
            src_ref=src, dst_ref=dst,
            send_sem=send_sem.at[phase, to], recv_sem=recv_sem.at[phase, slot_from],
            device_id=dev, device_id_type=pl.DeviceIdType.MESH,
        )

    started = []

    def send_p(phase, src, dst):
        for o in p_peers():
            c = copy(phase, src(o), dst(p), o, p, device(o, q))
            c.start()
            started.append(c)

    def send_q(phase, src, dst):
        for o in q_peers():
            c = copy(phase, src(o), dst(q), o, q, device(p, o))
            c.start()
            started.append(c)

    def wait_p(phase, dst):
        for o in p_peers():
            copy(phase, dst(o), dst(o), o, o, device(o, q)).wait_recv()

    def wait_q(phase, dst):
        for o in q_peers():
            copy(phase, dst(o), dst(o), o, o, device(p, o)).wait_recv()

    loads[0].wait()
    wire = basis_ref[...].astype(BF16)
    basis_rows(ga, q)[...] = wire
    basis_rows(gb, p)[...] = wire
    for c in loads[1:4]:
        c.wait()
    split_columns(lg_ref, lgs)
    lgr[p] = lgs[p]

    class Group:
        def __init__(self, index, buffer, ring, pair, where):
            self.index, self.buffer, self.ring, self.pair, self.where = index, buffer, ring, pair, where
            self.sent = 0

        def slot(self, step, other):
            pair = (1 - self.pair) if other else self.pair
            return ((self.ring + step) % 4) * 2 + pair

        def half(self, slot, h):
            return rows(self.buffer, slot * 2 + h, 16)

        def copy(self, slot, h, to, n):
            ref = self.half(slot, h)
            return pltpu.make_async_remote_copy(
                src_ref=ref, dst_ref=ref,
                send_sem=gather_send.at[self.index, n], recv_sem=gather_recv.at[self.index, slot * 2 + h],
                device_id=self.where(to), device_id_type=pl.DeviceIdType.MESH,
            )

        def send(self, slot, h, to):
            c = self.copy(slot, h, to, self.sent)
            self.sent += 1
            c.start()
            started.append(c)

        def wait(self, step, other, h):
            slot = self.slot(step, other)
            self.copy(slot, h, self.slot(0, True), 0).wait_recv()
            return slot

        def own(self):
            me_ = self.slot(0, False)
            after, before, partner = self.slot(1, False), self.slot(3, False), self.slot(0, True)
            self.send(me_, 0, after)
            self.send(me_, 1, before)
            self.send(me_, 0, partner)
            self.send(me_, 1, partner)
            self.send(me_, 0, before)
            self.send(me_, 1, after)

        def relay(self, other):
            self.send(self.wait(3, other, 0), 0, self.slot(1, False))
            self.send(self.wait(1, other, 1), 1, self.slot(3, False))

        def partner(self):
            slot = self.wait(0, True, 0)
            self.send(slot, 0, self.slot(1, False))
            self.send(slot, 0, self.slot(3, False))
            slot = self.wait(0, True, 1)
            self.send(slot, 1, self.slot(3, False))
            self.send(slot, 1, self.slot(1, False))

        def rest(self):
            for other in (False, True):
                self.wait(3, other, 1)
                self.wait(1, other, 0)
                self.wait(2, other, 0)
                self.wait(2, other, 1)

    by_q = Group(0, ga, z21, yh, lambda o: device(p, o))
    by_p = Group(1, gb, x, z0, lambda o: device(o, q))
    pl.semaphore_wait(barrier, 14)
    by_q.own()
    by_p.own()
    by_p.partner()
    send_p(LG, lambda o: lgs.at[o], lambda i: lgr.at[i])
    by_p.relay(False)
    by_q.relay(False)
    by_q.partner()
    by_p.relay(True)
    by_q.relay(True)
    by_p.rest()
    by_q.rest()
    wait_p(LG, lambda i: lgr.at[i])
    gram = dot(gb[:, :D], ga[:, :D], ((1,), (1,)))
    new = 0.95 * lgr[...].reshape(256, 256) + 0.05 * gram
    gn[...] = new.reshape(8, R, 256)
    gback[p] = gn[p]
    high = new.astype(BF16)
    rest = new - high.astype(F32)
    mid = rest.astype(BF16)
    low = (rest - mid.astype(F32)).astype(BF16)
    w = ga[:, D:]
    part = dot(high, w, ((1,), (0,))) + (dot(mid, w, ((1,), (0,))) + dot(low, w, ((1,), (0,))))
    pp[...] = part.reshape(8, R, K)
    send_p(PP, lambda o: pp.at[o], lambda i: pr.at[i])
    pr[p] = pp[p]
    wait_p(PP, lambda i: pr.at[i])

    def total(ref):
        s = ref[0]
        for i in range(1, 8):
            s = s + ref[i]
        return s

    own = total(pr)
    rows(pb, p)[...] = own
    send_p(PG, lambda o: rows(pb, p), lambda i: rows(pb, i))
    yc[...] = jnp.zeros_like(yc)
    call[:, K:] = jnp.zeros((K, 128), F32)
    call[:, K : K + R] = own.T
    wait_p(PG, lambda i: rows(pb, i))
    pt[...] = pb[...].T
    left = rows(pt, p, 64)[...]
    fp[...] = dot(left, pb[...], ((1,), (0,)), HIGHEST).reshape(8, 8, K)
    send_q(FR, lambda o: fp.at[o], lambda i: fr.at[i])
    send_p(GN, lambda o: gn.at[o], lambda i: gback.at[i])
    fr[q] = fp[q]
    cp[...] = dot(left, gb[:, D:].astype(F32), ((1,), (0,)), HIGHEST).reshape(8, 8, K)
    cr[q] = cp[q]

    def frow(i):
        return rows(fall, i, 64)

    def crow(i, n=8):
        return call.at[pl.ds(pl.multiple_of(i * n, n), n), pl.ds(0, K)]

    wait_q(FR, lambda i: fr.at[i])
    rows(fall, p * 8 + q, 8)[...] = total(fr)
    send_q(FA, lambda o: rows(fall, p * 8 + q, 8), lambda i: rows(fall, p * 8 + i, 8))
    wait_q(FA, lambda i: rows(fall, p * 8 + i, 8))
    send_p(FB, lambda o: frow(p), frow)
    send_q(CR, lambda o: cp.at[o], lambda i: cr.at[i])
    wait_p(GN, lambda i: gback.at[i])
    join_columns(gback, lgn_ref)

    def wait_row(phase, ref, i):
        @pl.when(i != p)
        def _():
            copy(phase, ref(i), ref(i), i, i, device(i, q)).wait_recv()

    scale = math.sqrt(D)

    def block(k):
        return slice(k * 128, (k + 1) * 128)

    def cross_reduced():
        wait_q(CR, lambda i: cr.at[i])
        crow(p * 8 + q)[...] = total(cr)
        send_q(CA, lambda o: crow(p * 8 + q), lambda i: crow(p * 8 + i))

    def cross_shared():
        wait_q(CA, lambda i: crow(p * 8 + i))
        send_p(CB, lambda o: crow(p, 64), lambda i: crow(i, 64))

    def side_rows(k):
        here = block(k)
        a = call[here, :]
        if k:
            a = a - dot3(yf[: k * 128, here], yc[: k * 128, :], ((0,), (0,)))
        y = dot3(inverse[k], a, ((1,), (0,)))
        yc[here, :] = y
        basis_out[:, here] = (scale * y[:, K:]).T[:R, :]
        rotation = y[:, :K] / scale
        avg_out[:, here] = dot3(avg_ref[...], rotation, ((1,), (1,)))
        sq_out[:, here] = dot3(sq_ref[...], rotation * rotation, ((1,), (1,)))

    hooks = {(0, 2): cross_reduced, (1, 0): cross_shared}
    for k in range(4):
        here = block(k)
        for i in (2 * k, 2 * k + 1):
            wait_row(FB, frow, i)
        if k == 3:
            for c in loads[4:]:
                c.wait()
            for i in (0, 1):
                wait_row(CB, lambda j: crow(j, 64), i)
        a = fall[here, k * 128 :]
        d = fall[here, here]
        if k:
            u = yf[: k * 128, here]
            d = d - dot(u, u, ((0,), (0,)), HIGHEST)
        diag[...] = d
        if k:
            a = a - dot(u, yf[: k * 128, k * 128 :], ((0,), (0,)), HIGHEST)
        if k == 3:
            side_rows(0)
        out = inverse_factor(
            [diag[8 * i : 8 * i + 8, :] for i in range(16)], {m: f for (j, m), f in hooks.items() if j == k}
        )
        for i in range(16):
            inverse[k, 8 * i : 8 * i + 8, :] = out[i]
        if k < 3:
            yf[here, k * 128 :] = dot(inverse[k], a, ((1,), (0,)), HIGHEST)
    for i in range(2, 8):
        wait_row(CB, lambda j: crow(j, 64), i)
    for k in (1, 2, 3):
        side_rows(k)
    for c in started:
        c.wait_send()


def body(grad, left_gram, basis, exp_avg, exp_avg_sq):
    vm = pl.BlockSpec(memory_space=pltpu.VMEM)
    sds = jax.ShapeDtypeStruct
    return pl.pallas_call(
        kernel,
        out_shape=(sds((R, D), F32), sds((R, K), F32), sds((R, K), F32), sds((R, K), F32)),
        in_specs=[pl.BlockSpec(memory_space=pltpu.HBM)] * 5,
        out_specs=(vm,) * 4,
        scratch_shapes=[
            pltpu.VMEM((R, D), F32), pltpu.VMEM((R, K), F32), pltpu.VMEM((R, K), F32), pltpu.VMEM((R, K), F32),
            pltpu.VMEM((256, WIDE), BF16), pltpu.VMEM((256, WIDE), BF16),
            pltpu.VMEM((8, R, 256), F32), pltpu.VMEM((8, R, 256), F32),
            pltpu.VMEM((8, R, 256), F32), pltpu.VMEM((8, R, 256), F32),
            pltpu.VMEM((8, R, K), F32), pltpu.VMEM((8, R, K), F32),
            pltpu.VMEM((256, K), F32), pltpu.VMEM((K, 256), F32),
            pltpu.VMEM((8, 8, K), F32), pltpu.VMEM((8, 8, K), F32),
            pltpu.VMEM((8, 8, K), F32), pltpu.VMEM((8, 8, K), F32),
            pltpu.VMEM((K, K), F32), pltpu.VMEM((K, K + 128), F32),
            pltpu.VMEM((K, K), F32), pltpu.VMEM((K, K + 128), F32),
            pltpu.VMEM((128, 128), F32), pltpu.VMEM((4, 128, 128), F32),
            pltpu.SemaphoreType.DMA((10, 8)), pltpu.SemaphoreType.DMA((10, 8)),
            pltpu.SemaphoreType.DMA((2, 14)), pltpu.SemaphoreType.DMA((2, 16)), pltpu.SemaphoreType.DMA((6,)),
        ],
        compiler_params=pltpu.CompilerParams(
            collective_id=0, has_side_effects=True, vmem_limit_bytes=48 * 1024 * 1024
        ),
        cost_estimate=pl.CostEstimate(flops=1_000_000_000, bytes_accessed=2_000_000, transcendentals=0),
        name="soap_refresh",
    )(grad, left_gram, basis, exp_avg, exp_avg_sq)


def solution(mesh):
    placed = P(("layer", "dp"), None)
    return jax.shard_map(
        body, mesh=mesh, in_specs=(placed,) * 5, out_specs=(placed,) * 4, check_vma=False
    )
```

```python
import functools
import math

import jax
import jax.numpy as jnp
from jax import lax
from jax.experimental import pallas as pl
from jax.experimental.pallas import tpu as pltpu
from jax.sharding import PartitionSpec as P

D = 2048
K = 512
R = 32
HIGHEST = lax.Precision.HIGHEST
F32 = jnp.float32
BF16 = jnp.bfloat16
LG, GN, PP, PG, R0, R1, A0, A1, FB, CR, CA, CB = 0, 1, 2, 3, 4, 5, 6, 7, 8, 12, 13, 14
WIDE = D + K


def dot(a, b, dims, precision=None):
    return lax.dot_general(a, b, (dims, ((), ())), precision=precision, preferred_element_type=F32)


def dot3(a, b, dims):
    ah, bh = a.astype(BF16), b.astype(BF16)
    al, bl = (a - ah.astype(F32)).astype(BF16), (b - bh.astype(F32)).astype(BF16)
    return dot(ah, bh, dims) + (dot(ah, bl, dims) + dot(al, bh, dims))


def lane(v, k):
    return jnp.broadcast_to(v[:, k : k + 1], (8, 128))


def sub(v, t):
    return jnp.broadcast_to(v[t : t + 1, :], (8, 128))


def inverse_factor(a_rows, hooks={}):
    row = lax.broadcasted_iota(jnp.int32, (8, 128), 0)
    col = lax.broadcasted_iota(jnp.int32, (8, 128), 1)
    n = len(a_rows)
    a_rows = list(a_rows)
    e_rows = [jnp.where(col == row + 8 * i, 1.0, 0.0).astype(F32) for i in range(n)]
    out = []
    for m in range(n):
        hooks.get(m, lambda: None)()
        r_m, s_m = a_rows[m], e_rows[m]
        c = [lane(r_m, 8 * m + t) for t in range(8)]
        v = jnp.zeros((8, 128), F32)
        for t in range(8):
            here = row == t
            pivot = sub(c[t], t)
            inv = 1.0 / pivot
            s_t = sub(s_m, t)
            v = jnp.where(here, s_t * lax.rsqrt(pivot), v)
            mult = jnp.where(here, -1.0, c[t])
            for u in range(t + 1, 8):
                c[u] = jnp.where(here, 0.0, c[u]) - (mult * sub(c[u], t)) * inv
            if m < n - 1:
                r_m = jnp.where(here, 0.0, r_m) - (mult * sub(r_m, t)) * inv
                s_m = jnp.where(here, 0.0, s_m) - (mult * s_t) * inv
            elif t < 7:
                s_m = jnp.where(here, 0.0, s_m) - (mult * s_t) * inv
        out.append(v)
        if m < n - 1:
            w = [sub(r_m, t) for t in range(8)]
            s = [sub(s_m, t) for t in range(8)]
            for i in range(m + 1, n):
                l = [lane(a_rows[i], 8 * m + t) for t in range(8)]
                for t in range(8):
                    a_rows[i] = a_rows[i] - l[t] * w[t]
                    e_rows[i] = e_rows[i] - l[t] * s[t]
    return out


def split_columns(lg_ref, out_ref):
    low = lax.broadcasted_iota(jnp.int32, (R, 128), 1) < 64
    for x in range(4):
        t = [lg_ref[:, x * 512 + k * 128 : x * 512 + (k + 1) * 128] for k in range(4)]
        for h in range(2):
            a, b = t[2 * h], t[2 * h + 1]
            out_ref[2 * x, :, h * 128 : (h + 1) * 128] = jnp.where(low, a, pltpu.roll(b, 64, 1))
            out_ref[2 * x + 1, :, h * 128 : (h + 1) * 128] = jnp.where(low, pltpu.roll(a, 64, 1), b)


def join_columns(in_ref, out_ref):
    low = lax.broadcasted_iota(jnp.int32, (R, 128), 1) < 64
    for x in range(4):
        for h in range(2):
            a = in_ref[2 * x, :, h * 128 : (h + 1) * 128]
            b = in_ref[2 * x + 1, :, h * 128 : (h + 1) * 128]
            at = x * 512 + h * 256
            out_ref[:, at : at + 128] = jnp.where(low, a, pltpu.roll(b, 64, 1))
            out_ref[:, at + 128 : at + 256] = jnp.where(low, pltpu.roll(a, 64, 1), b)


def kernel(
    grad_hbm, lg_hbm, basis_hbm, avg_hbm, sq_hbm,
    lgn_ref, basis_out, avg_out, sq_out,
    lg_ref, basis_ref, avg_ref, sq_ref,
    ga, gb, lgs, lgr, gn, gback, pp, pr, pb, pt, fp, fr, cp, cr, fa, fall, call, yf, yc, diag, inverse,
    send_sem, recv_sem, gather_send, gather_recv, in_sem,
):
    me = lax.axis_index("dp")
    x, z21, z0, yh = me // 16, (me // 4) % 4, (me // 2) % 2, me % 2
    p = x * 2 + z0
    q = z21 * 2 + yh

    def device(pp_, qq_):
        return {"dp": (pp_ // 2) * 16 + (qq_ // 2) * 4 + (pp_ % 2) * 2 + qq_ % 2}

    def p_peers():
        return [(p + d) % 8 for d in range(1, 8)]

    def q_peers():
        return [(q + d) % 8 for d in range(1, 8)]

    barrier = pltpu.get_barrier_semaphore()
    for o in p_peers():
        pl.semaphore_signal(barrier, inc=1, device_id=device(o, q), device_id_type=pl.DeviceIdType.MESH)
    for o in q_peers():
        pl.semaphore_signal(barrier, inc=1, device_id=device(p, o), device_id_type=pl.DeviceIdType.MESH)

    def rows(ref, i, n=R):
        return ref.at[pl.ds(pl.multiple_of(i * n, n), n)]

    def grad_rows(ref, i):
        return ref.at[pl.ds(pl.multiple_of(i * R, R), R), pl.ds(0, D)]

    def basis_rows(ref, i):
        return ref.at[pl.ds(pl.multiple_of(i * R, R), R), pl.ds(D, K)]

    loads = [
        pltpu.make_async_copy(basis_hbm, basis_ref, in_sem.at[0]),
        pltpu.make_async_copy(grad_hbm, grad_rows(ga, q), in_sem.at[1]),
        pltpu.make_async_copy(grad_hbm, grad_rows(gb, p), in_sem.at[2]),
        pltpu.make_async_copy(lg_hbm, lg_ref, in_sem.at[3]),
        pltpu.make_async_copy(avg_hbm, avg_ref, in_sem.at[4]),
        pltpu.make_async_copy(sq_hbm, sq_ref, in_sem.at[5]),
    ]
    for c in loads:
        c.start()

    def copy(phase, src, dst, to, slot_from, dev):
        return pltpu.make_async_remote_copy(
            src_ref=src, dst_ref=dst,
            send_sem=send_sem.at[phase, to], recv_sem=recv_sem.at[phase, slot_from],
            device_id=dev, device_id_type=pl.DeviceIdType.MESH,
        )

    started = []

    def send_p(phase, src, dst):
        for o in p_peers():
            c = copy(phase, src(o), dst(p), o, p, device(o, q))
            c.start()
            started.append(c)

    def send_q(phase, src, dst):
        for o in q_peers():
            c = copy(phase, src(o), dst(q), o, q, device(p, o))
            c.start()
            started.append(c)

    def wait_p(phase, dst):
        for o in p_peers():
            copy(phase, dst(o), dst(o), o, o, device(o, q)).wait_recv()

    def wait_q(phase, dst):
        for o in q_peers():
            copy(phase, dst(o), dst(o), o, o, device(p, o)).wait_recv()

    loads[0].wait()
    wire = basis_ref[...].astype(BF16)
    basis_rows(ga, q)[...] = wire
    basis_rows(gb, p)[...] = wire
    for c in loads[1:4]:
        c.wait()
    split_columns(lg_ref, lgs)
    lgr[p] = lgs[p]

    class Group:
        def __init__(self, index, buffer, ring, pair, where):
            self.index, self.buffer, self.ring, self.pair, self.where = index, buffer, ring, pair, where
            self.sent = 0

        def slot(self, step, other):
            pair = (1 - self.pair) if other else self.pair
            return ((self.ring + step) % 4) * 2 + pair

        def half(self, slot, h):
            return rows(self.buffer, slot * 2 + h, 16)

        def copy(self, slot, h, to, n):
            ref = self.half(slot, h)
            return pltpu.make_async_remote_copy(
                src_ref=ref, dst_ref=ref,
                send_sem=gather_send.at[self.index, n], recv_sem=gather_recv.at[self.index, slot * 2 + h],
                device_id=self.where(to), device_id_type=pl.DeviceIdType.MESH,
            )

        def send(self, slot, h, to):
            c = self.copy(slot, h, to, self.sent)
            self.sent += 1
            c.start()
            started.append(c)

        def wait(self, step, other, h):
            slot = self.slot(step, other)
            self.copy(slot, h, self.slot(0, True), 0).wait_recv()
            return slot

        def own(self):
            me_ = self.slot(0, False)
            after, before, partner = self.slot(1, False), self.slot(3, False), self.slot(0, True)
            self.send(me_, 0, after)
            self.send(me_, 1, before)
            self.send(me_, 0, partner)
            self.send(me_, 1, partner)
            self.send(me_, 0, before)
            self.send(me_, 1, after)

        def relay(self, other):
            self.send(self.wait(3, other, 0), 0, self.slot(1, False))
            self.send(self.wait(1, other, 1), 1, self.slot(3, False))

        def partner(self):
            slot = self.wait(0, True, 0)
            self.send(slot, 0, self.slot(1, False))
            self.send(slot, 0, self.slot(3, False))
            slot = self.wait(0, True, 1)
            self.send(slot, 1, self.slot(3, False))
            self.send(slot, 1, self.slot(1, False))

        def rest(self):
            for other in (False, True):
                self.wait(3, other, 1)
                self.wait(1, other, 0)
                self.wait(2, other, 0)
                self.wait(2, other, 1)

    by_q = Group(0, ga, z21, yh, lambda o: device(p, o))
    by_p = Group(1, gb, x, z0, lambda o: device(o, q))
    pl.semaphore_wait(barrier, 14)
    by_q.own()
    by_p.own()
    by_p.partner()
    send_p(LG, lambda o: lgs.at[o], lambda i: lgr.at[i])
    by_p.relay(False)
    by_q.relay(False)
    by_q.partner()
    by_p.relay(True)
    by_q.relay(True)
    by_p.rest()
    by_q.rest()
    wait_p(LG, lambda i: lgr.at[i])
    gram = dot(gb[:, :D], ga[:, :D], ((1,), (1,)))
    new = 0.95 * lgr[...].reshape(256, 256) + 0.05 * gram
    gn[...] = new.reshape(8, R, 256)
    gback[p] = gn[p]
    high = new.astype(BF16)
    rest = new - high.astype(F32)
    mid = rest.astype(BF16)
    low = (rest - mid.astype(F32)).astype(BF16)
    w = ga[:, D:]
    part = dot(high, w, ((1,), (0,))) + (dot(mid, w, ((1,), (0,))) + dot(low, w, ((1,), (0,))))
    pp[...] = part.reshape(8, R, K)
    send_p(PP, lambda o: pp.at[o], lambda i: pr.at[i])
    pr[p] = pp[p]
    wait_p(PP, lambda i: pr.at[i])

    def total(ref):
        s = ref[0]
        for i in range(1, 8):
            s = s + ref[i]
        return s

    own = total(pr)
    rows(pb, p)[...] = own
    send_p(PG, lambda o: rows(pb, p), lambda i: rows(pb, i))
    call[:, :, :, K:] = jnp.zeros((4, 8, 16, 128), F32)
    own_t = own.T
    for k in range(4):
        for i in range(8):
            at = k * 128 + i * 16
            call[k, i, :, K : K + R] = own_t[at : at + 16]
    wait_p(PG, lambda i: rows(pb, i))
    pt[...] = pb[...].T
    left = jnp.concatenate(
        [pt[pl.ds(pl.multiple_of(k * 128 + p * 16, 16), 16), :] for k in range(4)], axis=0
    )
    part = dot(left, pb[...], ((1,), (0,)), HIGHEST)

    def tiles(slot):
        h, j = slot // 4, slot % 4
        return [(0, h, j), (1, h, j + 1) if j < 3 else (3, h, 3), (2, h, 2 + j % 2)]

    for slot in range(8):
        for n, (k, h, c) in enumerate(tiles(slot)):
            fp[slot, n] = part[k * 16 + h * 8 : k * 16 + h * 8 + 8, c * 128 : c * 128 + 128]
    send_q(R0, lambda o: fp.at[o, pl.ds(0, 1)], lambda i: fr.at[i, pl.ds(0, 1)])
    send_q(R1, lambda o: fp.at[o, pl.ds(1, 2)], lambda i: fr.at[i, pl.ds(1, 2)])
    fr[q] = fp[q]
    cp[...] = dot(left, gb[:, D:].astype(F32), ((1,), (0,)), HIGHEST).reshape(8, 8, K)
    send_q(CR, lambda o: cp.at[o], lambda i: cr.at[i])
    cr[q] = cp[q]

    def frow(k):
        return lambda i: fall.at[k, i, :, pl.ds(k * 128, K - k * 128)]

    def c8(i):
        return call.at[i // 2, p, pl.ds(pl.multiple_of((i % 2) * 8, 8), 8), pl.ds(0, K)]

    def c64(i):
        return call.at[:, i, :, pl.ds(0, K)]

    wait_q(R0, lambda i: fr.at[i, pl.ds(0, 1)])
    fa[q, 0] = total(fr.at[:, 0])
    send_q(A0, lambda o: fa.at[q, pl.ds(0, 1)], lambda i: fa.at[i, pl.ds(0, 1)])
    wait_q(R1, lambda i: fr.at[i, pl.ds(1, 2)])
    for n in (1, 2):
        fa[q, n] = total(fr.at[:, n])
    send_q(A1, lambda o: fa.at[q, pl.ds(1, 2)], lambda i: fa.at[i, pl.ds(1, 2)])
    send_p(GN, lambda o: gn.at[o], lambda i: gback.at[i])

    def place(numbers):
        for slot in range(8):
            for n, (k, h, c) in enumerate(tiles(slot)):
                if n in numbers and not (n == 2 and slot % 4 > 1):
                    fall[k, p, h * 8 : h * 8 + 8, c * 128 : c * 128 + 128] = fa[slot, n]

    wait_q(A0, lambda i: fa.at[i, pl.ds(0, 1)])
    place((0,))
    send_p(FB, lambda o: frow(0)(p), frow(0))
    wait_q(A1, lambda i: fa.at[i, pl.ds(1, 2)])
    place((1, 2))
    for k in (1, 2, 3):
        send_p(FB + k, lambda o: frow(k)(p), frow(k))
    wait_q(CR, lambda i: cr.at[i])
    c8(q)[...] = total(cr)
    send_q(CA, lambda o: c8(q), c8)
    wait_p(GN, lambda i: gback.at[i])
    join_columns(gback, lgn_ref)

    scale = math.sqrt(D)

    def block(k):
        return slice(k * 128, (k + 1) * 128)

    def cross_shared():
        wait_q(CA, c8)
        send_p(CB, lambda o: c64(p), c64)

    def side_rows(k):
        here = block(k)
        a = call[k].reshape(128, K + 128)
        if k:
            a = a - dot3(yf[: k * 128, here], yc[: k * 128, :], ((0,), (0,)))
        y = dot3(inverse[k], a, ((1,), (0,)))
        yc[here, :] = y
        basis_out[:, here] = (scale * y[:, K:]).T[:R, :]
        rotation = y[:, :K] / scale
        avg_out[:, here] = dot3(avg_ref[...], rotation, ((1,), (1,)))
        sq_out[:, here] = dot3(sq_ref[...], rotation * rotation, ((1,), (1,)))

    def side_early():
        for c in loads[4:]:
            c.wait()
        wait_p(CB, c64)
        for k in (0, 1, 2):
            side_rows(k)

    hooks = {(0, 6): cross_shared, (3, 4): side_early}
    for k in range(4):
        here = block(k)
        wait_p(FB + k, frow(k))
        a = fall[k, :, :, k * 128 :].reshape(128, K - k * 128)
        d = a[:, :128]
        if k:
            u = yf[: k * 128, here]
            d = d - dot(u, u, ((0,), (0,)), HIGHEST)
        diag[...] = d
        if k:
            a = a - dot(u, yf[: k * 128, k * 128 :], ((0,), (0,)), HIGHEST)
        out = inverse_factor(
            [diag[8 * i : 8 * i + 8, :] for i in range(16)], {m: f for (j, m), f in hooks.items() if j == k}
        )
        for i in range(16):
            inverse[k, 8 * i : 8 * i + 8, :] = out[i]
        if k < 3:
            yf[here, k * 128 :] = dot(inverse[k], a, ((1,), (0,)), HIGHEST)
    side_rows(3)
    for c in started:
        c.wait_send()


def body(grad, left_gram, basis, exp_avg, exp_avg_sq):
    vm = pl.BlockSpec(memory_space=pltpu.VMEM)
    sds = jax.ShapeDtypeStruct
    return pl.pallas_call(
        kernel,
        out_shape=(sds((R, D), F32), sds((R, K), F32), sds((R, K), F32), sds((R, K), F32)),
        in_specs=[pl.BlockSpec(memory_space=pltpu.HBM)] * 5,
        out_specs=(vm,) * 4,
        scratch_shapes=[
            pltpu.VMEM((R, D), F32), pltpu.VMEM((R, K), F32), pltpu.VMEM((R, K), F32), pltpu.VMEM((R, K), F32),
            pltpu.VMEM((256, WIDE), BF16), pltpu.VMEM((256, WIDE), BF16),
            pltpu.VMEM((8, R, 256), F32), pltpu.VMEM((8, R, 256), F32),
            pltpu.VMEM((8, R, 256), F32), pltpu.VMEM((8, R, 256), F32),
            pltpu.VMEM((8, R, K), F32), pltpu.VMEM((8, R, K), F32),
            pltpu.VMEM((256, K), F32), pltpu.VMEM((K, 256), F32),
            pltpu.VMEM((8, 3, 8, 128), F32), pltpu.VMEM((8, 3, 8, 128), F32),
            pltpu.VMEM((8, 8, K), F32), pltpu.VMEM((8, 8, K), F32),
            pltpu.VMEM((8, 3, 8, 128), F32),
            pltpu.VMEM((4, 8, 16, K), F32), pltpu.VMEM((4, 8, 16, K + 128), F32),
            pltpu.VMEM((K, K), F32), pltpu.VMEM((K, K + 128), F32),
            pltpu.VMEM((128, 128), F32), pltpu.VMEM((4, 128, 128), F32),
            pltpu.SemaphoreType.DMA((15, 8)), pltpu.SemaphoreType.DMA((15, 8)),
            pltpu.SemaphoreType.DMA((2, 14)), pltpu.SemaphoreType.DMA((2, 16)), pltpu.SemaphoreType.DMA((6,)),
        ],
        compiler_params=pltpu.CompilerParams(
            collective_id=0, has_side_effects=True, vmem_limit_bytes=60 * 1024 * 1024
        ),
        cost_estimate=pl.CostEstimate(flops=1_000_000_000, bytes_accessed=2_000_000, transcendentals=0),
        name="soap_refresh",
    )(grad, left_gram, basis, exp_avg, exp_avg_sq)


def solution(mesh):
    placed = P(("layer", "dp"), None)
    return jax.shard_map(
        body, mesh=mesh, in_specs=(placed,) * 5, out_specs=(placed,) * 4, check_vma=False
    )
```

```python
import functools
import math

import jax
import jax.numpy as jnp
from jax import lax
from jax.experimental import pallas as pl
from jax.experimental.pallas import tpu as pltpu
from jax.sharding import PartitionSpec as P

D = 2048
K = 512
R = 32
HIGHEST = lax.Precision.HIGHEST
F32 = jnp.float32
BF16 = jnp.bfloat16
LG, GN, PP, PG, R0, R1, A0, A1, FB, CR, CA, CB = 0, 1, 2, 4, 6, 7, 8, 9, 10, 14, 15, 16
WIDE = D + K


def dot(a, b, dims, precision=None):
    return lax.dot_general(a, b, (dims, ((), ())), precision=precision, preferred_element_type=F32)


def dot3(a, b, dims):
    ah, bh = a.astype(BF16), b.astype(BF16)
    al, bl = (a - ah.astype(F32)).astype(BF16), (b - bh.astype(F32)).astype(BF16)
    return dot(ah, bh, dims) + (dot(ah, bl, dims) + dot(al, bh, dims))


def lane(v, k):
    return jnp.broadcast_to(v[:, k : k + 1], (8, 128))


def sub(v, t):
    return jnp.broadcast_to(v[t : t + 1, :], (8, 128))


def inverse_factor(a_rows, hooks={}):
    row = lax.broadcasted_iota(jnp.int32, (8, 128), 0)
    col = lax.broadcasted_iota(jnp.int32, (8, 128), 1)
    n = len(a_rows)
    a_rows = list(a_rows)
    e_rows = [jnp.where(col == row + 8 * i, 1.0, 0.0).astype(F32) for i in range(n)]
    out = []
    for m in range(n):
        hooks.get(m, lambda: None)()
        r_m, s_m = a_rows[m], e_rows[m]
        c = [lane(r_m, 8 * m + t) for t in range(8)]
        v = jnp.zeros((8, 128), F32)
        for t in range(0, 8, 2):
            first, second, both = row == t, row == t + 1, row // 2 == t // 2
            d00, d10, d11 = sub(c[t], t), sub(c[t], t + 1), sub(c[t + 1], t + 1)
            det = d00 * d11 - d10 * d10
            inv = 1.0 / det
            m0 = jnp.where(first, -1.0, jnp.where(second, 0.0, c[t]))
            m1 = jnp.where(first, 0.0, jnp.where(second, -1.0, c[t + 1]))
            f0, f1 = m0 * d11 - m1 * d10, m1 * d00 - m0 * d10
            s0, s1 = sub(s_m, t), sub(s_m, t + 1)
            root = lax.rsqrt(d00)
            v = jnp.where(first, s0 * root, v)
            v = jnp.where(second, (d00 * s1 - d10 * s0) * (root * lax.rsqrt(det)), v)

            def step(x, x0, x1):
                return jnp.where(both, 0.0, x) - (f0 * x0 + f1 * x1) * inv

            for u in range(t + 2, 8):
                c[u] = step(c[u], sub(c[u], t), sub(c[u], t + 1))
            if m < n - 1:
                r_m = step(r_m, sub(r_m, t), sub(r_m, t + 1))
            if m < n - 1 or t < 6:
                s_m = step(s_m, s0, s1)
        out.append(v)
        if m < n - 1:
            w = [sub(r_m, t) for t in range(8)]
            s = [sub(s_m, t) for t in range(8)]
            for i in range(m + 1, n):
                l = [lane(a_rows[i], 8 * m + t) for t in range(8)]
                for t in range(8):
                    a_rows[i] = a_rows[i] - l[t] * w[t]
                    e_rows[i] = e_rows[i] - l[t] * s[t]
    return out


def split_columns(lg_ref, out_ref):
    low = lax.broadcasted_iota(jnp.int32, (R, 128), 1) < 64
    for x in range(4):
        t = [lg_ref[:, x * 512 + k * 128 : x * 512 + (k + 1) * 128] for k in range(4)]
        for h in range(2):
            a, b = t[2 * h], t[2 * h + 1]
            out_ref[2 * x, :, h * 128 : (h + 1) * 128] = jnp.where(low, a, pltpu.roll(b, 64, 1))
            out_ref[2 * x + 1, :, h * 128 : (h + 1) * 128] = jnp.where(low, pltpu.roll(a, 64, 1), b)


def join_columns(in_ref, out_ref):
    low = lax.broadcasted_iota(jnp.int32, (R, 128), 1) < 64
    for x in range(4):
        for h in range(2):
            a = in_ref[2 * x, :, h * 128 : (h + 1) * 128]
            b = in_ref[2 * x + 1, :, h * 128 : (h + 1) * 128]
            at = x * 512 + h * 256
            out_ref[:, at : at + 128] = jnp.where(low, a, pltpu.roll(b, 64, 1))
            out_ref[:, at + 128 : at + 256] = jnp.where(low, pltpu.roll(a, 64, 1), b)


def kernel(
    grad_hbm, lg_hbm, basis_hbm, avg_hbm, sq_hbm,
    out_ref,
    lg_ref, basis_ref, avg_ref, sq_ref,
    ga, gb, lgs, lgr, gn, gback, pp, pr, pb, pt, fp, fr, cp, cr, fa, fall, call, yf, yc, diag, inverse, avg_t, sq_t,
    send_sem, recv_sem, gather_send, gather_recv, in_sem,
):
    lgn_ref = out_ref.at[:, pl.ds(0, D)]
    basis_out, avg_out, sq_out = [out_ref.at[:, pl.ds(D + i * K, K)] for i in range(3)]
    me = lax.axis_index("dp")
    x, z21, z0, yh = me // 16, (me // 4) % 4, (me // 2) % 2, me % 2
    p = x * 2 + z0
    q = z21 * 2 + yh

    def device(pp_, qq_):
        return {"dp": (pp_ // 2) * 16 + (qq_ // 2) * 4 + (pp_ % 2) * 2 + qq_ % 2}

    def p_peers():
        return [(p + d) % 8 for d in range(1, 8)]

    def q_peers():
        return [(q + d) % 8 for d in range(1, 8)]

    barrier = pltpu.get_barrier_semaphore()
    for o in p_peers():
        pl.semaphore_signal(barrier, inc=1, device_id=device(o, q), device_id_type=pl.DeviceIdType.MESH)
    for o in q_peers():
        pl.semaphore_signal(barrier, inc=1, device_id=device(p, o), device_id_type=pl.DeviceIdType.MESH)

    def rows(ref, i, n=R):
        return ref.at[pl.ds(pl.multiple_of(i * n, n), n)]

    def grad_rows(ref, i):
        return ref.at[pl.ds(pl.multiple_of(i * R, R), R), pl.ds(0, D)]

    def basis_rows(ref, i):
        return ref.at[pl.ds(pl.multiple_of(i * R, R), R), pl.ds(D, K)]

    loads = [
        pltpu.make_async_copy(basis_hbm, basis_ref, in_sem.at[0]),
        pltpu.make_async_copy(grad_hbm, grad_rows(ga, q), in_sem.at[1]),
        pltpu.make_async_copy(grad_hbm, grad_rows(gb, p), in_sem.at[2]),
        pltpu.make_async_copy(lg_hbm, lg_ref, in_sem.at[3]),
        pltpu.make_async_copy(avg_hbm, avg_ref, in_sem.at[4]),
        pltpu.make_async_copy(sq_hbm, sq_ref, in_sem.at[5]),
    ]
    for c in loads:
        c.start()

    def copy(phase, src, dst, to, slot_from, dev):
        return pltpu.make_async_remote_copy(
            src_ref=src, dst_ref=dst,
            send_sem=send_sem.at[phase, to], recv_sem=recv_sem.at[phase, slot_from],
            device_id=dev, device_id_type=pl.DeviceIdType.MESH,
        )

    started = []

    def send_p(phase, src, dst):
        for o in p_peers():
            c = copy(phase, src(o), dst(p), o, p, device(o, q))
            c.start()
            started.append(c)

    def send_q(phase, src, dst):
        for o in q_peers():
            c = copy(phase, src(o), dst(q), o, q, device(p, o))
            c.start()
            started.append(c)

    def wait_p(phase, dst):
        for o in p_peers():
            copy(phase, dst(o), dst(o), o, o, device(o, q)).wait_recv()

    def wait_q(phase, dst):
        for o in q_peers():
            copy(phase, dst(o), dst(o), o, o, device(p, o)).wait_recv()

    loads[0].wait()
    wire = basis_ref[...].astype(BF16)
    basis_rows(ga, q)[...] = wire
    basis_rows(gb, p)[...] = wire
    for c in loads[1:3]:
        c.wait()

    class Group:
        def __init__(self, index, buffer, ring, pair, where):
            self.index, self.buffer, self.ring, self.pair, self.where = index, buffer, ring, pair, where
            self.sent = 0

        def slot(self, step, other):
            pair = (1 - self.pair) if other else self.pair
            return ((self.ring + step) % 4) * 2 + pair

        def half(self, slot, h):
            return rows(self.buffer, slot * 2 + h, 16)

        def copy(self, slot, h, to, n):
            ref = self.half(slot, h)
            return pltpu.make_async_remote_copy(
                src_ref=ref, dst_ref=ref,
                send_sem=gather_send.at[self.index, n], recv_sem=gather_recv.at[self.index, slot * 2 + h],
                device_id=self.where(to), device_id_type=pl.DeviceIdType.MESH,
            )

        def send(self, slot, h, to):
            c = self.copy(slot, h, to, self.sent)
            self.sent += 1
            c.start()
            started.append(c)

        def wait(self, step, other, h):
            slot = self.slot(step, other)
            self.copy(slot, h, self.slot(0, True), 0).wait_recv()
            return slot

        def own(self):
            me_ = self.slot(0, False)
            after, before, partner = self.slot(1, False), self.slot(3, False), self.slot(0, True)
            self.send(me_, 0, after)
            self.send(me_, 1, before)
            self.send(me_, 0, partner)
            self.send(me_, 1, partner)
            self.send(me_, 0, before)
            self.send(me_, 1, after)

        def relay_top(self):
            self.send(self.wait(3, True, 0), 0, self.slot(1, False))

        def across(self):
            self.send(self.wait(2, False, 1), 1, self.slot(0, True))

        def relay(self, other):
            self.send(self.wait(3, other, 0), 0, self.slot(1, False))
            self.send(self.wait(1, other, 1), 1, self.slot(3, False))

        def partner(self):
            slot = self.wait(0, True, 0)
            self.send(slot, 0, self.slot(1, False))
            self.send(slot, 0, self.slot(3, False))
            slot = self.wait(0, True, 1)
            self.send(slot, 1, self.slot(3, False))
            self.send(slot, 1, self.slot(1, False))

        def rest(self, crossed):
            for other in (False, True):
                self.wait(3, other, 1)
                self.wait(1, other, 0)
                self.wait(2, other, 0)
                if other and crossed:
                    self.wait(1, other, 1)
                if other or not crossed:
                    self.wait(2, other, 1)

    by_q = Group(0, ga, z21, yh, lambda o: device(p, o))
    by_p = Group(1, gb, x, z0, lambda o: device(o, q))
    pl.semaphore_wait(barrier, 14)
    by_q.own()
    by_p.own()
    by_p.partner()
    loads[3].wait()
    split_columns(lg_ref, lgs)
    lgr[p] = lgs[p]
    send_p(LG, lambda o: lgs.at[o], lambda i: lgr.at[i])
    by_p.relay(False)
    by_q.relay(False)
    by_q.partner()
    by_q.across()
    by_p.relay(True)
    by_q.relay_top()
    by_p.rest(False)
    by_q.rest(True)
    wait_p(LG, lambda i: lgr.at[i])
    gram = dot(gb[:, :D], ga[:, :D], ((1,), (1,)))
    new = 0.95 * lgr[...].reshape(256, 256) + 0.05 * gram
    gn[...] = new.reshape(8, R, 256)
    gback[p] = gn[p]
    high = new.astype(BF16)
    rest = new - high.astype(F32)
    mid = rest.astype(BF16)
    low = (rest - mid.astype(F32)).astype(BF16)
    def total(ref):
        s = ref[0]
        for i in range(1, 8):
            s = s + ref[i]
        return s

    def half(ref, i, h):
        return ref.at[i, :, pl.ds(h * 256, 256)]

    def rows_half(i, h):
        return pb.at[pl.ds(pl.multiple_of(i * R, R), R), pl.ds(h * 256, 256)]

    for h in range(2):
        w = ga[:, D + h * 256 : D + h * 256 + 256]
        part = dot(high, w, ((1,), (0,))) + (dot(mid, w, ((1,), (0,))) + dot(low, w, ((1,), (0,))))
        pp[:, :, h * 256 : h * 256 + 256] = part.reshape(8, R, 256)
        send_p(PP + h, lambda o: half(pp, o, h), lambda i: half(pr, i, h))
    pr[p] = pp[p]
    for h in range(2):
        wait_p(PP + h, lambda i: half(pr, i, h))
        rows_half(p, h)[...] = total(pr.at[:, :, pl.ds(h * 256, 256)])
        send_p(PG + h, lambda o: rows_half(p, h), lambda i: rows_half(i, h))
    own = rows(pb, p)[...]
    call[:, :, :, K:] = jnp.zeros((4, 8, 16, 128), F32)
    own_t = own.T
    for k in range(4):
        for i in range(8):
            at = k * 128 + i * 16
            call[k, i, :, K : K + R] = own_t[at : at + 16]
    for h in range(2):
        wait_p(PG + h, lambda i: rows_half(i, h))
        pt[h * 256 : h * 256 + 256, :] = pb[:, h * 256 : h * 256 + 256].T
    left = jnp.concatenate(
        [pt[pl.ds(pl.multiple_of(k * 128 + p * 16, 16), 16), :] for k in range(4)], axis=0
    )
    part = dot(left, pb[...], ((1,), (0,)), HIGHEST)

    def tiles(slot):
        h, j = slot // 4, slot % 4
        return [(0, h, j), (1, h, j + 1) if j < 3 else (3, h, 3), (2, h, 2 + j % 2)]

    for slot in range(8):
        for n, (k, h, c) in enumerate(tiles(slot)):
            fp[slot, n] = part[k * 16 + h * 8 : k * 16 + h * 8 + 8, c * 128 : c * 128 + 128]
    send_q(R0, lambda o: fp.at[o, pl.ds(0, 1)], lambda i: fr.at[i, pl.ds(0, 1)])
    send_q(R1, lambda o: fp.at[o, pl.ds(1, 2)], lambda i: fr.at[i, pl.ds(1, 2)])
    fr[q] = fp[q]
    cp[...] = dot(left, gb[:, D:].astype(F32), ((1,), (0,)), HIGHEST).reshape(8, 8, K)
    send_q(CR, lambda o: cp.at[o], lambda i: cr.at[i])
    cr[q] = cp[q]

    def frow(k):
        return lambda i: fall.at[k, i, :, pl.ds(k * 128, K - k * 128)]

    def c8(i):
        return call.at[i // 2, p, pl.ds(pl.multiple_of((i % 2) * 8, 8), 8), pl.ds(0, K)]

    def crows(i):
        return call.at[:, i, :, pl.ds(0, K)]

    wait_q(R0, lambda i: fr.at[i, pl.ds(0, 1)])
    fa[q, 0] = total(fr.at[:, 0])
    send_q(A0, lambda o: fa.at[q, pl.ds(0, 1)], lambda i: fa.at[i, pl.ds(0, 1)])
    wait_q(R1, lambda i: fr.at[i, pl.ds(1, 2)])
    for n in (1, 2):
        fa[q, n] = total(fr.at[:, n])
    send_q(A1, lambda o: fa.at[q, pl.ds(1, 2)], lambda i: fa.at[i, pl.ds(1, 2)])
    send_p(GN, lambda o: gn.at[o], lambda i: gback.at[i])

    def place(numbers):
        for slot in range(8):
            for n, (k, h, c) in enumerate(tiles(slot)):
                if n in numbers and not (n == 2 and slot % 4 > 1):
                    fall[k, p, h * 8 : h * 8 + 8, c * 128 : c * 128 + 128] = fa[slot, n]

    wait_q(A0, lambda i: fa.at[i, pl.ds(0, 1)])
    place((0,))
    send_p(FB, lambda o: frow(0)(p), frow(0))
    wait_q(A1, lambda i: fa.at[i, pl.ds(1, 2)])
    place((1, 2))
    for k in (1, 2, 3):
        send_p(FB + k, lambda o: frow(k)(p), frow(k))
    wait_q(CR, lambda i: cr.at[i])
    c8(q)[...] = total(cr)
    send_q(CA, lambda o: c8(q), c8)
    for c in loads[4:]:
        c.wait()
    wait_p(GN, lambda i: gback.at[i])
    join_columns(gback, lgn_ref)
    for source, turned in ((avg_ref, avg_t), (sq_ref, sq_t)):
        turned[...] = jnp.zeros((K, 128), F32)
        turned[:, :R] = source[...].T

    scale = math.sqrt(D)

    def block(k):
        return slice(k * 128, (k + 1) * 128)

    def cross_shared():
        for k in (1, 2, 3):
            wait_p(FB + k, frow(k))
        wait_q(CA, c8)
        send_p(CB, lambda o: crows(p), crows)

    def tile_of(k, first, last):
        return fall[k, :, :, first * 128 : last * 128].reshape(128, (last - first) * 128) * unit

    state = {}

    def side_before(k):
        here = block(k)
        a = call[k].reshape(128, K + 128)
        if k:
            a = a - dot3(yf[: k * 128, here], yc[: k * 128, :], ((0,), (0,)))
        yc[here, :] = a

    def side_after(k):
        here = block(k)
        y = dot3(inverse[k], yc[here, :], ((1,), (0,)))
        yc[here, :] = y
        basis_out[:, here] = (y[:, K:] * (scale * root)).T[:R, :]
        rotation = y[:, :K] * (root / scale)
        avg_out[:, here] = dot3(rotation, avg_t[...], ((1,), (0,))).T[:R, :]
        sq_out[:, here] = dot3(rotation * rotation, sq_t[...], ((1,), (0,))).T[:R, :]

    def side():
        wait_p(CB, crows)
        for k in range(3):
            side_before(k)
            side_after(k)
        side_before(3)

    def wide(k):
        def run():
            if k < 3:
                yf[block(k - 1), (k + 1) * 128 :] = dot(inverse[k - 1], state["a"][:, 128:], ((1,), (0,)), HIGHEST)
                u = yf[: k * 128, block(k)]
                state["a"] = tile_of(k, k + 1, 4) - dot(u, yf[: k * 128, (k + 1) * 128 :], ((0,), (0,)), HIGHEST)
                v = yf[: k * 128, block(k + 1)]
                state["d"] = tile_of(k + 1, k + 1, k + 2) - dot(v, v, ((0,), (0,)), HIGHEST)
        return run

    hooks = {
        (0, 6): cross_shared, (1, 2): wide(1), (2, 2): wide(2),
        (3, 4): side,
    }
    wait_p(FB, frow(0))
    unit = 1.0 / fall[0, 0, 0:1, 0:1]
    root = jnp.sqrt(unit)
    diag[...] = tile_of(0, 0, 1)
    for k in range(4):
        here = block(k)
        out = inverse_factor(
            [diag[8 * i : 8 * i + 8, :] for i in range(16)], {m: f for (j, m), f in hooks.items() if j == k}
        )
        for i in range(16):
            inverse[k, 8 * i : 8 * i + 8, :] = out[i]
        if k < 3:
            if k == 0:
                state["a"], state["d"] = tile_of(0, 1, 4), tile_of(1, 1, 2)
            t = dot(inverse[k], state["a"][:, :128], ((1,), (0,)), HIGHEST)
            yf[here, block(k + 1)] = t
            diag[...] = state["d"] - dot(t, t, ((0,), (0,)), HIGHEST)
    side_after(3)
    for c in started:
        c.wait_send()


def body(grad, left_gram, basis, exp_avg, exp_avg_sq):
    vm = pl.BlockSpec(memory_space=pltpu.VMEM)
    sds = jax.ShapeDtypeStruct
    both = pl.pallas_call(
        kernel,
        out_shape=sds((R, D + 3 * K), F32),
        in_specs=[pl.BlockSpec(memory_space=pltpu.HBM)] * 5,
        out_specs=vm,
        scratch_shapes=[
            pltpu.VMEM((R, D), F32), pltpu.VMEM((R, K), F32), pltpu.VMEM((R, K), F32), pltpu.VMEM((R, K), F32),
            pltpu.VMEM((256, WIDE), BF16), pltpu.VMEM((256, WIDE), BF16),
            pltpu.VMEM((8, R, 256), F32), pltpu.VMEM((8, R, 256), F32),
            pltpu.VMEM((8, R, 256), F32), pltpu.VMEM((8, R, 256), F32),
            pltpu.VMEM((8, R, K), F32), pltpu.VMEM((8, R, K), F32),
            pltpu.VMEM((256, K), F32), pltpu.VMEM((K, 256), F32),
            pltpu.VMEM((8, 3, 8, 128), F32), pltpu.VMEM((8, 3, 8, 128), F32),
            pltpu.VMEM((8, 8, K), F32), pltpu.VMEM((8, 8, K), F32),
            pltpu.VMEM((8, 3, 8, 128), F32),
            pltpu.VMEM((4, 8, 16, K), F32), pltpu.VMEM((4, 8, 16, K + 128), F32),
            pltpu.VMEM((K, K), F32), pltpu.VMEM((K, K + 128), F32),
            pltpu.VMEM((128, 128), F32), pltpu.VMEM((4, 128, 128), F32),
            pltpu.VMEM((K, 128), F32), pltpu.VMEM((K, 128), F32),
            pltpu.SemaphoreType.DMA((20, 8)), pltpu.SemaphoreType.DMA((20, 8)),
            pltpu.SemaphoreType.DMA((2, 14)), pltpu.SemaphoreType.DMA((2, 16)), pltpu.SemaphoreType.DMA((6,)),
        ],
        compiler_params=pltpu.CompilerParams(
            collective_id=0, has_side_effects=True, vmem_limit_bytes=60 * 1024 * 1024
        ),
        cost_estimate=pl.CostEstimate(flops=1_000_000_000, bytes_accessed=2_000_000, transcendentals=0),
        name="soap_refresh",
    )(grad, left_gram, basis, exp_avg, exp_avg_sq)
    return (both[:, :D],) + tuple(both[:, D + i * K : D + i * K + K] for i in range(3))


def solution(mesh):
    placed = P(("layer", "dp"), None)
    return jax.shard_map(
        body, mesh=mesh, in_specs=(placed,) * 5, out_specs=(placed,) * 4, check_vma=False
    )
```

```python
import functools
import math

import jax
import jax.numpy as jnp
from jax import lax
from jax.experimental import pallas as pl
from jax.experimental.pallas import tpu as pltpu
from jax.sharding import PartitionSpec as P

D = 2048
K = 512
R = 32
HIGHEST = lax.Precision.HIGHEST
F32 = jnp.float32
BF16 = jnp.bfloat16
LG, GN, PP, PG, R0, R1, A0, A1, FB, CR, CA, CB = 0, 1, 2, 4, 6, 7, 8, 9, 10, 14, 15, 16
WIDE = D + K


def dot(a, b, dims, precision=None):
    return lax.dot_general(a, b, (dims, ((), ())), precision=precision, preferred_element_type=F32)


def dot3(a, b, dims):
    ah, bh = a.astype(BF16), b.astype(BF16)
    al, bl = (a - ah.astype(F32)).astype(BF16), (b - bh.astype(F32)).astype(BF16)
    return dot(ah, bh, dims) + (dot(ah, bl, dims) + dot(al, bh, dims))


def lane(v, k):
    return jnp.broadcast_to(v[:, k : k + 1], (8, 128))


def sub(v, t):
    return jnp.broadcast_to(v[t : t + 1, :], (8, 128))


def inverse_factor(a_rows, hooks={}):
    row = lax.broadcasted_iota(jnp.int32, (8, 128), 0)
    col = lax.broadcasted_iota(jnp.int32, (8, 128), 1)
    n = len(a_rows)
    a_rows = list(a_rows)
    e_rows = [jnp.where(col == row + 8 * i, 1.0, 0.0).astype(F32) for i in range(n)]
    out = []
    for m in range(n):
        hooks.get(m, lambda: None)()
        r_m, s_m = a_rows[m], e_rows[m]
        c = [lane(r_m, 8 * m + t) for t in range(8)]
        v = jnp.zeros((8, 128), F32)
        for t in range(0, 8, 2):
            first, second, both = row == t, row == t + 1, row // 2 == t // 2
            d00, d10, d11 = sub(c[t], t), sub(c[t], t + 1), sub(c[t + 1], t + 1)
            det = d00 * d11 - d10 * d10
            inv = 1.0 / det
            m0 = jnp.where(first, -1.0, jnp.where(second, 0.0, c[t]))
            m1 = jnp.where(first, 0.0, jnp.where(second, -1.0, c[t + 1]))
            f0, f1 = m0 * d11 - m1 * d10, m1 * d00 - m0 * d10
            s0, s1 = sub(s_m, t), sub(s_m, t + 1)
            root = lax.rsqrt(d00)
            v = jnp.where(first, s0 * root, v)
            v = jnp.where(second, (d00 * s1 - d10 * s0) * (root * lax.rsqrt(det)), v)

            def step(x, x0, x1):
                return jnp.where(both, 0.0, x) - (f0 * x0 + f1 * x1) * inv

            for u in range(t + 2, 8):
                c[u] = step(c[u], sub(c[u], t), sub(c[u], t + 1))
            if m < n - 1:
                r_m = step(r_m, sub(r_m, t), sub(r_m, t + 1))
            if m < n - 1 or t < 6:
                s_m = step(s_m, s0, s1)
        out.append(v)
        if m < n - 1:
            w = [sub(r_m, t) for t in range(8)]
            s = [sub(s_m, t) for t in range(8)]
            for i in range(m + 1, n):
                l = [lane(a_rows[i], 8 * m + t) for t in range(8)]
                for t in range(8):
                    a_rows[i] = a_rows[i] - l[t] * w[t]
                    e_rows[i] = e_rows[i] - l[t] * s[t]
    return out


def split_columns(lg_ref, out_ref):
    low = lax.broadcasted_iota(jnp.int32, (R, 128), 1) < 64
    for x in range(4):
        t = [lg_ref[:, x * 512 + k * 128 : x * 512 + (k + 1) * 128] for k in range(4)]
        for h in range(2):
            a, b = t[2 * h], t[2 * h + 1]
            out_ref[2 * x, :, h * 128 : (h + 1) * 128] = jnp.where(low, a, pltpu.roll(b, 64, 1))
            out_ref[2 * x + 1, :, h * 128 : (h + 1) * 128] = jnp.where(low, pltpu.roll(a, 64, 1), b)


def join_columns(in_ref, out_ref):
    low = lax.broadcasted_iota(jnp.int32, (R, 128), 1) < 64
    for x in range(4):
        for h in range(2):
            a = in_ref[2 * x, :, h * 128 : (h + 1) * 128]
            b = in_ref[2 * x + 1, :, h * 128 : (h + 1) * 128]
            at = x * 512 + h * 256
            out_ref[:, at : at + 128] = jnp.where(low, a, pltpu.roll(b, 64, 1))
            out_ref[:, at + 128 : at + 256] = jnp.where(low, pltpu.roll(a, 64, 1), b)


def kernel(
    grad_hbm, lg_hbm, basis_hbm, avg_hbm, sq_hbm,
    out_ref,
    lg_ref, basis_ref, avg_ref, sq_ref,
    ga, gb, lgs, lgr, gn, gback, pp, pr, pb, pt, fp, fr, cp, cr, fa, fall, call, yf, yc, diag, inverse, avg_t, sq_t,
    send_sem, recv_sem, gather_send, gather_recv, in_sem,
):
    lgn_ref = out_ref.at[:, pl.ds(0, D)]
    basis_out, avg_out, sq_out = [out_ref.at[:, pl.ds(D + i * K, K)] for i in range(3)]
    me = lax.axis_index("dp")
    x, z21, z0, yh = me // 16, (me // 4) % 4, (me // 2) % 2, me % 2
    p = x * 2 + z0
    q = z21 * 2 + yh

    def device(pp_, qq_):
        return {"dp": (pp_ // 2) * 16 + (qq_ // 2) * 4 + (pp_ % 2) * 2 + qq_ % 2}

    def p_peers():
        return [(p + d) % 8 for d in range(1, 8)]

    def q_peers():
        return [(q + d) % 8 for d in range(1, 8)]

    barrier = pltpu.get_barrier_semaphore()
    for o in p_peers():
        pl.semaphore_signal(barrier, inc=1, device_id=device(o, q), device_id_type=pl.DeviceIdType.MESH)
    for o in q_peers():
        pl.semaphore_signal(barrier, inc=1, device_id=device(p, o), device_id_type=pl.DeviceIdType.MESH)

    def rows(ref, i, n=R):
        return ref.at[pl.ds(pl.multiple_of(i * n, n), n)]

    def grad_rows(ref, i):
        return ref.at[pl.ds(pl.multiple_of(i * R, R), R), pl.ds(0, D)]

    def basis_rows(ref, i):
        return ref.at[pl.ds(pl.multiple_of(i * R, R), R), pl.ds(D, K)]

    loads = [
        pltpu.make_async_copy(basis_hbm, basis_ref, in_sem.at[0]),
        pltpu.make_async_copy(grad_hbm, grad_rows(ga, q), in_sem.at[1]),
        pltpu.make_async_copy(grad_hbm, grad_rows(gb, p), in_sem.at[2]),
        pltpu.make_async_copy(lg_hbm, lg_ref, in_sem.at[3]),
        pltpu.make_async_copy(avg_hbm, avg_ref, in_sem.at[4]),
        pltpu.make_async_copy(sq_hbm, sq_ref, in_sem.at[5]),
    ]
    for c in loads:
        c.start()

    def copy(phase, src, dst, to, slot_from, dev):
        return pltpu.make_async_remote_copy(
            src_ref=src, dst_ref=dst,
            send_sem=send_sem.at[phase, to], recv_sem=recv_sem.at[phase, slot_from],
            device_id=dev, device_id_type=pl.DeviceIdType.MESH,
        )

    started = []

    def send_p(phase, src, dst):
        for o in p_peers():
            c = copy(phase, src(o), dst(p), o, p, device(o, q))
            c.start()
            started.append(c)

    def send_q(phase, src, dst):
        for o in q_peers():
            c = copy(phase, src(o), dst(q), o, q, device(p, o))
            c.start()
            started.append(c)

    def wait_p(phase, dst):
        for o in p_peers():
            copy(phase, dst(o), dst(o), o, o, device(o, q)).wait_recv()

    def wait_q(phase, dst):
        for o in q_peers():
            copy(phase, dst(o), dst(o), o, o, device(p, o)).wait_recv()

    loads[0].wait()
    wire = basis_ref[...].astype(BF16)
    basis_rows(ga, q)[...] = wire
    basis_rows(gb, p)[...] = wire
    for c in loads[1:3]:
        c.wait()

    class Group:
        def __init__(self, index, buffer, ring, pair, where):
            self.index, self.buffer, self.ring, self.pair, self.where = index, buffer, ring, pair, where
            self.sent = 0

        def slot(self, step, other):
            pair = (1 - self.pair) if other else self.pair
            return ((self.ring + step) % 4) * 2 + pair

        def half(self, slot, h):
            return rows(self.buffer, slot * 2 + h, 16)

        def copy(self, slot, h, to, n):
            ref = self.half(slot, h)
            return pltpu.make_async_remote_copy(
                src_ref=ref, dst_ref=ref,
                send_sem=gather_send.at[self.index, n], recv_sem=gather_recv.at[self.index, slot * 2 + h],
                device_id=self.where(to), device_id_type=pl.DeviceIdType.MESH,
            )

        def send(self, slot, h, to):
            c = self.copy(slot, h, to, self.sent)
            self.sent += 1
            c.start()
            started.append(c)

        def wait(self, step, other, h):
            slot = self.slot(step, other)
            self.copy(slot, h, self.slot(0, True), 0).wait_recv()
            return slot

        def own(self):
            me_ = self.slot(0, False)
            after, before, partner = self.slot(1, False), self.slot(3, False), self.slot(0, True)
            self.send(me_, 0, after)
            self.send(me_, 1, before)
            self.send(me_, 0, partner)
            self.send(me_, 1, partner)
            self.send(me_, 0, before)
            self.send(me_, 1, after)

        def across(self, h):
            self.send(self.wait(2, False, h), h, self.slot(0, True))

        def relay(self, other):
            self.send(self.wait(3, other, 0), 0, self.slot(1, False))
            self.send(self.wait(1, other, 1), 1, self.slot(3, False))

        def partner(self, h):
            slot = self.wait(0, True, h)
            self.send(slot, h, self.slot(1 + 2 * h, False))
            self.send(slot, h, self.slot(3 - 2 * h, False))

        def rest(self, crossed):
            for other in (False, True):
                self.wait(3, other, 1)
                self.wait(1, other, 0)
                if other and crossed:
                    self.wait(3, other, 0)
                    self.wait(1, other, 1)
                if other or not crossed:
                    self.wait(2, other, 0)
                    self.wait(2, other, 1)

    by_q = Group(0, ga, z21, yh, lambda o: device(p, o))
    by_p = Group(1, gb, x, z0, lambda o: device(o, q))
    pl.semaphore_wait(barrier, 14)
    by_q.own()
    by_p.own()
    by_q.relay(False)
    by_p.partner(0)
    by_p.partner(1)
    loads[3].wait()
    split_columns(lg_ref, lgs)
    lgr[p] = lgs[p]
    send_p(LG, lambda o: lgs.at[o], lambda i: lgr.at[i])
    by_p.relay(False)
    by_q.partner(0)
    by_p.relay(True)
    by_q.across(0)
    by_q.partner(1)
    by_q.across(1)
    by_p.rest(False)
    by_q.rest(True)
    wait_p(LG, lambda i: lgr.at[i])
    gram = dot(gb[:, :D], ga[:, :D], ((1,), (1,)))
    new = 0.95 * lgr[...].reshape(256, 256) + 0.05 * gram
    gn[...] = new.reshape(8, R, 256)
    gback[p] = gn[p]
    high = new.astype(BF16)
    rest = new - high.astype(F32)
    mid = rest.astype(BF16)
    low = (rest - mid.astype(F32)).astype(BF16)
    def total(ref):
        s = ref[0]
        for i in range(1, 8):
            s = s + ref[i]
        return s

    def half(ref, i, h):
        return ref.at[i, :, pl.ds(h * 256, 256)]

    def rows_half(i, h):
        return pb.at[pl.ds(pl.multiple_of(i * R, R), R), pl.ds(h * 256, 256)]

    for h in range(2):
        w = ga[:, D + h * 256 : D + h * 256 + 256]
        part = dot(high, w, ((1,), (0,))) + (dot(mid, w, ((1,), (0,))) + dot(low, w, ((1,), (0,))))
        pp[:, :, h * 256 : h * 256 + 256] = part.reshape(8, R, 256)
        send_p(PP + h, lambda o: half(pp, o, h), lambda i: half(pr, i, h))
    pr[p] = pp[p]
    for h in range(2):
        wait_p(PP + h, lambda i: half(pr, i, h))
        rows_half(p, h)[...] = total(pr.at[:, :, pl.ds(h * 256, 256)])
        send_p(PG + h, lambda o: rows_half(p, h), lambda i: rows_half(i, h))
    own = rows(pb, p)[...]
    call[:, :, :, K:] = jnp.zeros((4, 8, 16, 128), F32)
    own_t = own.T
    for k in range(4):
        for i in range(8):
            at = k * 128 + i * 16
            call[k, i, :, K : K + R] = own_t[at : at + 16]
    for h in range(2):
        wait_p(PG + h, lambda i: rows_half(i, h))
        pt[h * 256 : h * 256 + 256, :] = pb[:, h * 256 : h * 256 + 256].T
    left = jnp.concatenate(
        [pt[pl.ds(pl.multiple_of(k * 128 + p * 16, 16), 16), :] for k in range(4)], axis=0
    )
    part = dot(left, pb[...], ((1,), (0,)), HIGHEST)

    def tiles(slot):
        h, j = slot // 4, slot % 4
        return [(0, h, j), (1, h, j + 1) if j < 3 else (3, h, 3), (2, h, 2 + j % 2)]

    for slot in range(8):
        for n, (k, h, c) in enumerate(tiles(slot)):
            fp[slot, n] = part[k * 16 + h * 8 : k * 16 + h * 8 + 8, c * 128 : c * 128 + 128]
    send_q(R0, lambda o: fp.at[o, pl.ds(0, 1)], lambda i: fr.at[i, pl.ds(0, 1)])
    send_q(R1, lambda o: fp.at[o, pl.ds(1, 2)], lambda i: fr.at[i, pl.ds(1, 2)])
    fr[q] = fp[q]
    cp[...] = dot(left, gb[:, D:].astype(F32), ((1,), (0,)), HIGHEST).reshape(8, 8, K)
    send_q(CR, lambda o: cp.at[o], lambda i: cr.at[i])
    cr[q] = cp[q]

    def frow(k):
        return lambda i: fall.at[k, i, :, pl.ds(k * 128, K - k * 128)]

    def c8(i):
        return call.at[i // 2, p, pl.ds(pl.multiple_of((i % 2) * 8, 8), 8), pl.ds(0, K)]

    def crows(h):
        return lambda i: call.at[pl.ds(2 * h, 2), i, :, pl.ds(0, K)]

    wait_q(R0, lambda i: fr.at[i, pl.ds(0, 1)])
    fa[q, 0] = total(fr.at[:, 0])
    send_q(A0, lambda o: fa.at[q, pl.ds(0, 1)], lambda i: fa.at[i, pl.ds(0, 1)])
    wait_q(R1, lambda i: fr.at[i, pl.ds(1, 2)])
    for n in (1, 2):
        fa[q, n] = total(fr.at[:, n])
    send_q(A1, lambda o: fa.at[q, pl.ds(1, 2)], lambda i: fa.at[i, pl.ds(1, 2)])
    send_p(GN, lambda o: gn.at[o], lambda i: gback.at[i])

    def place(numbers):
        for slot in range(8):
            for n, (k, h, c) in enumerate(tiles(slot)):
                if n in numbers and not (n == 2 and slot % 4 > 1):
                    fall[k, p, h * 8 : h * 8 + 8, c * 128 : c * 128 + 128] = fa[slot, n]

    wait_q(A0, lambda i: fa.at[i, pl.ds(0, 1)])
    place((0,))
    send_p(FB, lambda o: frow(0)(p), frow(0))
    wait_q(CR, lambda i: cr.at[i])
    c8(q)[...] = total(cr)
    send_q(CA, lambda o: c8(q), c8)
    wait_q(A1, lambda i: fa.at[i, pl.ds(1, 2)])
    place((1, 2))
    for k in (1, 2, 3):
        send_p(FB + k, lambda o: frow(k)(p), frow(k))
    for c in loads[4:]:
        c.wait()
    wait_p(GN, lambda i: gback.at[i])
    join_columns(gback, lgn_ref)
    for source, turned in ((avg_ref, avg_t), (sq_ref, sq_t)):
        turned[...] = jnp.zeros((K, 128), F32)
        turned[:, :R] = source[...].T

    scale = math.sqrt(D)

    def block(k):
        return slice(k * 128, (k + 1) * 128)

    def cross_shared():
        for k in (1, 2, 3):
            wait_p(FB + k, frow(k))
        wait_q(CA, c8)
        for h in range(2):
            send_p(CB + h, lambda o: crows(h)(p), crows(h))

    def tile_of(k, first, last):
        return fall[k, :, :, first * 128 : last * 128].reshape(128, (last - first) * 128) * unit

    state = {}

    def side_before(k):
        here = block(k)
        a = call[k].reshape(128, K + 128)
        if k:
            a = a - dot3(yf[: k * 128, here], yc[: k * 128, :], ((0,), (0,)))
        yc[here, :] = a

    def side_after(k):
        here = block(k)
        y = dot3(inverse[k], yc[here, :], ((1,), (0,)))
        yc[here, :] = y
        basis_out[:, here] = (y[:, K:] * (scale * root)).T[:R, :]
        rotation = y[:, :K] * (root / scale)
        avg_out[:, here] = dot3(rotation, avg_t[...], ((1,), (0,))).T[:R, :]
        sq_out[:, here] = dot3(rotation * rotation, sq_t[...], ((1,), (0,))).T[:R, :]

    def side(h):
        def run():
            wait_p(CB + h, crows(h))
            side_before(2 * h)
            side_after(2 * h)
            side_before(2 * h + 1)
            if h == 0:
                side_after(1)
        return run

    def wide(k):
        def run():
            if k < 3:
                yf[block(k - 1), (k + 1) * 128 :] = dot(inverse[k - 1], state["a"][:, 128:], ((1,), (0,)), HIGHEST)
                u = yf[: k * 128, block(k)]
                state["a"] = tile_of(k, k + 1, 4) - dot(u, yf[: k * 128, (k + 1) * 128 :], ((0,), (0,)), HIGHEST)
                v = yf[: k * 128, block(k + 1)]
                state["d"] = tile_of(k + 1, k + 1, k + 2) - dot(v, v, ((0,), (0,)), HIGHEST)
        return run

    hooks = {
        (0, 6): cross_shared, (1, 2): wide(1), (2, 2): wide(2),
        (3, 2): side(0), (3, 9): side(1),
    }
    wait_p(FB, frow(0))
    unit = 1.0 / fall[0, 0, 0:1, 0:1]
    root = jnp.sqrt(unit)
    diag[...] = tile_of(0, 0, 1)
    for k in range(4):
        here = block(k)
        out = inverse_factor(
            [diag[8 * i : 8 * i + 8, :] for i in range(16)], {m: f for (j, m), f in hooks.items() if j == k}
        )
        for i in range(16):
            inverse[k, 8 * i : 8 * i + 8, :] = out[i]
        if k < 3:
            if k == 0:
                state["a"], state["d"] = tile_of(0, 1, 4), tile_of(1, 1, 2)
            t = dot(inverse[k], state["a"][:, :128], ((1,), (0,)), HIGHEST)
            yf[here, block(k + 1)] = t
            diag[...] = state["d"] - dot(t, t, ((0,), (0,)), HIGHEST)
    side_after(3)
    for c in started:
        c.wait_send()


def body(grad, left_gram, basis, exp_avg, exp_avg_sq):
    vm = pl.BlockSpec(memory_space=pltpu.VMEM)
    sds = jax.ShapeDtypeStruct
    both = pl.pallas_call(
        kernel,
        out_shape=sds((R, D + 3 * K), F32),
        in_specs=[pl.BlockSpec(memory_space=pltpu.HBM)] * 5,
        out_specs=vm,
        scratch_shapes=[
            pltpu.VMEM((R, D), F32), pltpu.VMEM((R, K), F32), pltpu.VMEM((R, K), F32), pltpu.VMEM((R, K), F32),
            pltpu.VMEM((256, WIDE), BF16), pltpu.VMEM((256, WIDE), BF16),
            pltpu.VMEM((8, R, 256), F32), pltpu.VMEM((8, R, 256), F32),
            pltpu.VMEM((8, R, 256), F32), pltpu.VMEM((8, R, 256), F32),
            pltpu.VMEM((8, R, K), F32), pltpu.VMEM((8, R, K), F32),
            pltpu.VMEM((256, K), F32), pltpu.VMEM((K, 256), F32),
            pltpu.VMEM((8, 3, 8, 128), F32), pltpu.VMEM((8, 3, 8, 128), F32),
            pltpu.VMEM((8, 8, K), F32), pltpu.VMEM((8, 8, K), F32),
            pltpu.VMEM((8, 3, 8, 128), F32),
            pltpu.VMEM((4, 8, 16, K), F32), pltpu.VMEM((4, 8, 16, K + 128), F32),
            pltpu.VMEM((K, K), F32), pltpu.VMEM((K, K + 128), F32),
            pltpu.VMEM((128, 128), F32), pltpu.VMEM((4, 128, 128), F32),
            pltpu.VMEM((K, 128), F32), pltpu.VMEM((K, 128), F32),
            pltpu.SemaphoreType.DMA((20, 8)), pltpu.SemaphoreType.DMA((20, 8)),
            pltpu.SemaphoreType.DMA((2, 14)), pltpu.SemaphoreType.DMA((2, 16)), pltpu.SemaphoreType.DMA((6,)),
        ],
        compiler_params=pltpu.CompilerParams(
            collective_id=0, has_side_effects=True, vmem_limit_bytes=60 * 1024 * 1024
        ),
        cost_estimate=pl.CostEstimate(flops=1_000_000_000, bytes_accessed=2_000_000, transcendentals=0),
        name="soap_refresh",
    )(grad, left_gram, basis, exp_avg, exp_avg_sq)
    return (both[:, :D],) + tuple(both[:, D + i * K : D + i * K + K] for i in range(3))


def solution(mesh):
    placed = P(("layer", "dp"), None)
    return jax.shard_map(
        body, mesh=mesh, in_specs=(placed,) * 5, out_specs=(placed,) * 4, check_vma=False
    )
```

```python
import functools
import math

import jax
import jax.numpy as jnp
from jax import lax
from jax.experimental import pallas as pl
from jax.experimental.pallas import tpu as pltpu
from jax.sharding import PartitionSpec as P

D = 2048
K = 512
R = 32
HIGHEST = lax.Precision.HIGHEST
F32 = jnp.float32
BF16 = jnp.bfloat16
LG, GN, PP, PG, R0, R1, A0, A1, FB, CR, CA, CB = 0, 1, 2, 4, 6, 7, 8, 9, 10, 14, 15, 16
WIDE = D + K


def dot(a, b, dims, precision=None):
    return lax.dot_general(a, b, (dims, ((), ())), precision=precision, preferred_element_type=F32)


def dot3(a, b, dims):
    ah, bh = a.astype(BF16), b.astype(BF16)
    al, bl = (a - ah.astype(F32)).astype(BF16), (b - bh.astype(F32)).astype(BF16)
    return dot(ah, bh, dims) + (dot(ah, bl, dims) + dot(al, bh, dims))


def lane(v, k):
    return jnp.broadcast_to(v[:, k : k + 1], (8, 128))


def sub(v, t):
    return jnp.broadcast_to(v[t : t + 1, :], (8, 128))


def inverse_factor(a_rows, hooks={}):
    row = lax.broadcasted_iota(jnp.int32, (8, 128), 0)
    col = lax.broadcasted_iota(jnp.int32, (8, 128), 1)
    n = len(a_rows)
    a_rows = list(a_rows)
    e_rows = [jnp.where(col == row + 8 * i, 1.0, 0.0).astype(F32) for i in range(n)]
    out = []
    for m in range(n):
        hooks.get(m, lambda: None)()
        r_m, s_m = a_rows[m], e_rows[m]
        c = [lane(r_m, 8 * m + t) for t in range(8)]
        v = jnp.zeros((8, 128), F32)
        for t in range(0, 8, 2):
            first, second, both = row == t, row == t + 1, row // 2 == t // 2
            d00, d10, d11 = sub(c[t], t), sub(c[t], t + 1), sub(c[t + 1], t + 1)
            det = d00 * d11 - d10 * d10
            inv = 1.0 / det
            m0 = jnp.where(first, -1.0, jnp.where(second, 0.0, c[t]))
            m1 = jnp.where(first, 0.0, jnp.where(second, -1.0, c[t + 1]))
            f0, f1 = m0 * d11 - m1 * d10, m1 * d00 - m0 * d10
            s0, s1 = sub(s_m, t), sub(s_m, t + 1)
            root = lax.rsqrt(d00)
            v = jnp.where(first, s0 * root, v)
            v = jnp.where(second, (d00 * s1 - d10 * s0) * (root * lax.rsqrt(det)), v)

            def step(x, x0, x1):
                return jnp.where(both, 0.0, x) - (f0 * x0 + f1 * x1) * inv

            for u in range(t + 2, 8):
                c[u] = step(c[u], sub(c[u], t), sub(c[u], t + 1))
            if m < n - 1:
                r_m = step(r_m, sub(r_m, t), sub(r_m, t + 1))
            if m < n - 1 or t < 6:
                s_m = step(s_m, s0, s1)
        out.append(v)
        if m < n - 1:
            w = [sub(r_m, t) for t in range(8)]
            s = [sub(s_m, t) for t in range(8)]
            for i in range(m + 1, n):
                l = [lane(a_rows[i], 8 * m + t) for t in range(8)]
                for t in range(8):
                    a_rows[i] = a_rows[i] - l[t] * w[t]
                    e_rows[i] = e_rows[i] - l[t] * s[t]
    return out


def split_columns(lg_ref, out_ref):
    low = lax.broadcasted_iota(jnp.int32, (R, 128), 1) < 64
    for x in range(4):
        t = [lg_ref[:, x * 512 + k * 128 : x * 512 + (k + 1) * 128] for k in range(4)]
        for h in range(2):
            a, b = t[2 * h], t[2 * h + 1]
            out_ref[2 * x, :, h * 128 : (h + 1) * 128] = jnp.where(low, a, pltpu.roll(b, 64, 1))
            out_ref[2 * x + 1, :, h * 128 : (h + 1) * 128] = jnp.where(low, pltpu.roll(a, 64, 1), b)


def join_columns(in_ref, out_ref):
    low = lax.broadcasted_iota(jnp.int32, (R, 128), 1) < 64
    for x in range(4):
        for h in range(2):
            a = in_ref[2 * x, :, h * 128 : (h + 1) * 128]
            b = in_ref[2 * x + 1, :, h * 128 : (h + 1) * 128]
            at = x * 512 + h * 256
            out_ref[:, at : at + 128] = jnp.where(low, a, pltpu.roll(b, 64, 1))
            out_ref[:, at + 128 : at + 256] = jnp.where(low, pltpu.roll(a, 64, 1), b)


def kernel(
    grad_hbm, lg_hbm, basis_hbm, avg_hbm, sq_hbm,
    out_ref,
    lg_ref, basis_ref, avg_ref, sq_ref,
    ga, gb, lgs, lgr, gn, gback, pp, pr, pb, pt, fp, fr, cp, cr, fa, fall, call, yf, yc, diag, inverse, avg_t, sq_t,
    send_sem, recv_sem, gather_send, gather_recv, in_sem,
):
    lgn_ref = out_ref.at[:, pl.ds(0, D)]
    basis_out, avg_out, sq_out = [out_ref.at[:, pl.ds(D + i * K, K)] for i in range(3)]
    me = lax.axis_index("dp")
    x, z21, z0, yh = me // 16, (me // 4) % 4, (me // 2) % 2, me % 2
    p = x * 2 + z0
    q = z21 * 2 + yh

    def device(pp_, qq_):
        return {"dp": (pp_ // 2) * 16 + (qq_ // 2) * 4 + (pp_ % 2) * 2 + qq_ % 2}

    def p_peers():
        return [(p + d) % 8 for d in range(1, 8)]

    def q_peers():
        return [(q + d) % 8 for d in range(1, 8)]

    barrier = pltpu.get_barrier_semaphore()
    for o in p_peers():
        pl.semaphore_signal(barrier, inc=1, device_id=device(o, q), device_id_type=pl.DeviceIdType.MESH)
    for o in q_peers():
        pl.semaphore_signal(barrier, inc=1, device_id=device(p, o), device_id_type=pl.DeviceIdType.MESH)

    def rows(ref, i, n=R):
        return ref.at[pl.ds(pl.multiple_of(i * n, n), n)]

    def grad_rows(ref, i):
        return ref.at[pl.ds(pl.multiple_of(i * R, R), R), pl.ds(0, D)]

    def basis_rows(ref, i):
        return ref.at[pl.ds(pl.multiple_of(i * R, R), R), pl.ds(D, K)]

    loads = [
        pltpu.make_async_copy(basis_hbm, basis_ref, in_sem.at[0]),
        pltpu.make_async_copy(grad_hbm, grad_rows(ga, q), in_sem.at[1]),
        pltpu.make_async_copy(grad_hbm, grad_rows(gb, p), in_sem.at[2]),
        pltpu.make_async_copy(lg_hbm, lg_ref, in_sem.at[3]),
        pltpu.make_async_copy(avg_hbm, avg_ref, in_sem.at[4]),
        pltpu.make_async_copy(sq_hbm, sq_ref, in_sem.at[5]),
    ]
    for c in loads:
        c.start()

    def copy(phase, src, dst, to, slot_from, dev):
        return pltpu.make_async_remote_copy(
            src_ref=src, dst_ref=dst,
            send_sem=send_sem.at[phase, to], recv_sem=recv_sem.at[phase, slot_from],
            device_id=dev, device_id_type=pl.DeviceIdType.MESH,
        )

    started = []

    def send_p(phase, src, dst):
        for o in p_peers():
            c = copy(phase, src(o), dst(p), o, p, device(o, q))
            c.start()
            started.append(c)

    def send_q(phase, src, dst):
        for o in q_peers():
            c = copy(phase, src(o), dst(q), o, q, device(p, o))
            c.start()
            started.append(c)

    def wait_p(phase, dst):
        for o in p_peers():
            copy(phase, dst(o), dst(o), o, o, device(o, q)).wait_recv()

    def wait_q(phase, dst):
        for o in q_peers():
            copy(phase, dst(o), dst(o), o, o, device(p, o)).wait_recv()

    loads[0].wait()
    wire = basis_ref[...].astype(BF16)
    basis_rows(ga, q)[...] = wire
    basis_rows(gb, p)[...] = wire
    for c in loads[1:3]:
        c.wait()

    class Group:
        def __init__(self, index, buffer, ring, pair, where):
            self.index, self.buffer, self.ring, self.pair, self.where = index, buffer, ring, pair, where
            self.sent = 0

        def slot(self, step, other):
            pair = (1 - self.pair) if other else self.pair
            return ((self.ring + step) % 4) * 2 + pair

        def half(self, slot, h):
            return rows(self.buffer, slot * 2 + h, 16)

        def copy(self, slot, h, to, n):
            ref = self.half(slot, h)
            return pltpu.make_async_remote_copy(
                src_ref=ref, dst_ref=ref,
                send_sem=gather_send.at[self.index, n], recv_sem=gather_recv.at[self.index, slot * 2 + h],
                device_id=self.where(to), device_id_type=pl.DeviceIdType.MESH,
            )

        def send(self, slot, h, to):
            c = self.copy(slot, h, to, self.sent)
            self.sent += 1
            c.start()
            started.append(c)

        def wait(self, step, other, h):
            slot = self.slot(step, other)
            self.copy(slot, h, self.slot(0, True), 0).wait_recv()
            return slot

        def own(self):
            me_ = self.slot(0, False)
            after, before, partner = self.slot(1, False), self.slot(3, False), self.slot(0, True)
            self.send(me_, 0, partner)
            self.send(me_, 0, after)
            self.send(me_, 1, before)
            self.send(me_, 1, partner)
            self.send(me_, 0, before)
            self.send(me_, 1, after)

        def across(self, h):
            self.send(self.wait(2, False, h), h, self.slot(0, True))

        def relay(self, other):
            self.send(self.wait(3, other, 0), 0, self.slot(1, False))
            self.send(self.wait(1, other, 1), 1, self.slot(3, False))

        def partner(self, h):
            slot = self.wait(0, True, h)
            self.send(slot, h, self.slot(1 + 2 * h, False))
            self.send(slot, h, self.slot(3 - 2 * h, False))

        def rest(self, crossed):
            for other in (False, True):
                self.wait(3, other, 1)
                self.wait(1, other, 0)
                if other and crossed:
                    self.wait(3, other, 0)
                    self.wait(1, other, 1)
                if other or not crossed:
                    self.wait(2, other, 0)
                    self.wait(2, other, 1)

    by_q = Group(0, ga, z21, yh, lambda o: device(p, o))
    by_p = Group(1, gb, x, z0, lambda o: device(o, q))
    pl.semaphore_wait(barrier, 14)
    by_q.own()
    by_p.own()
    by_q.relay(False)
    by_p.partner(0)
    by_p.partner(1)
    loads[3].wait()
    split_columns(lg_ref, lgs)
    lgr[p] = lgs[p]
    send_p(LG, lambda o: lgs.at[o], lambda i: lgr.at[i])
    by_p.relay(False)
    by_q.partner(0)
    by_p.relay(True)
    by_q.across(0)
    by_q.partner(1)
    by_q.across(1)
    by_p.rest(False)
    by_q.rest(True)
    wait_p(LG, lambda i: lgr.at[i])
    gram = dot(gb[:, :D], ga[:, :D], ((1,), (1,)))
    new = 0.95 * lgr[...].reshape(256, 256) + 0.05 * gram
    gn[...] = new.reshape(8, R, 256)
    gback[p] = gn[p]
    high = new.astype(BF16)
    rest = new - high.astype(F32)
    mid = rest.astype(BF16)
    low = (rest - mid.astype(F32)).astype(BF16)
    def total(ref):
        s = ref[0]
        for i in range(1, 8):
            s = s + ref[i]
        return s

    def half(ref, i, h):
        return ref.at[i, :, pl.ds(h * 256, 256)]

    def rows_half(i, h):
        return pb.at[pl.ds(pl.multiple_of(i * R, R), R), pl.ds(h * 256, 256)]

    for h in range(2):
        w = ga[:, D + h * 256 : D + h * 256 + 256]
        part = dot(high, w, ((1,), (0,))) + (dot(mid, w, ((1,), (0,))) + dot(low, w, ((1,), (0,))))
        pp[:, :, h * 256 : h * 256 + 256] = part.reshape(8, R, 256)
        send_p(PP + h, lambda o: half(pp, o, h), lambda i: half(pr, i, h))
    pr[p] = pp[p]
    for h in range(2):
        wait_p(PP + h, lambda i: half(pr, i, h))
        rows_half(p, h)[...] = total(pr.at[:, :, pl.ds(h * 256, 256)])
        send_p(PG + h, lambda o: rows_half(p, h), lambda i: rows_half(i, h))
    own = rows(pb, p)[...]
    call[:, :, :, K:] = jnp.zeros((4, 8, 16, 128), F32)
    own_t = own.T
    for k in range(4):
        for i in range(8):
            at = k * 128 + i * 16
            call[k, i, :, K : K + R] = own_t[at : at + 16]
    for h in range(2):
        wait_p(PG + h, lambda i: rows_half(i, h))
        pt[h * 256 : h * 256 + 256, :] = pb[:, h * 256 : h * 256 + 256].T
    left = jnp.concatenate(
        [pt[pl.ds(pl.multiple_of(k * 128 + p * 16, 16), 16), :] for k in range(4)], axis=0
    )
    part = dot(left, pb[...], ((1,), (0,)), HIGHEST)

    def tiles(slot):
        h, j = slot // 4, slot % 4
        return [(0, h, j), (1, h, j + 1) if j < 3 else (3, h, 3), (2, h, 2 + j % 2)]

    for slot in range(8):
        for n, (k, h, c) in enumerate(tiles(slot)):
            fp[slot, n] = part[k * 16 + h * 8 : k * 16 + h * 8 + 8, c * 128 : c * 128 + 128]
    send_q(R0, lambda o: fp.at[o, pl.ds(0, 1)], lambda i: fr.at[i, pl.ds(0, 1)])
    send_q(R1, lambda o: fp.at[o, pl.ds(1, 2)], lambda i: fr.at[i, pl.ds(1, 2)])
    fr[q] = fp[q]
    cp[...] = dot(left, gb[:, D:].astype(F32), ((1,), (0,)), HIGHEST).reshape(8, 8, K)
    cr[q] = cp[q]

    def frow(k):
        return lambda i: fall.at[k, i, :, pl.ds(k * 128, K - k * 128)]

    def c8(i):
        return call.at[i // 2, p, pl.ds(pl.multiple_of((i % 2) * 8, 8), 8), pl.ds(0, K)]

    def crows(h):
        return lambda i: call.at[pl.ds(2 * h, 2), i, :, pl.ds(0, K)]

    wait_q(R0, lambda i: fr.at[i, pl.ds(0, 1)])
    fa[q, 0] = total(fr.at[:, 0])
    send_q(A0, lambda o: fa.at[q, pl.ds(0, 1)], lambda i: fa.at[i, pl.ds(0, 1)])
    send_q(CR, lambda o: cp.at[o], lambda i: cr.at[i])
    wait_q(R1, lambda i: fr.at[i, pl.ds(1, 2)])
    for n in (1, 2):
        fa[q, n] = total(fr.at[:, n])
    send_q(A1, lambda o: fa.at[q, pl.ds(1, 2)], lambda i: fa.at[i, pl.ds(1, 2)])
    send_p(GN, lambda o: gn.at[o], lambda i: gback.at[i])

    def place(numbers):
        for slot in range(8):
            for n, (k, h, c) in enumerate(tiles(slot)):
                if n in numbers and not (n == 2 and slot % 4 > 1):
                    fall[k, p, h * 8 : h * 8 + 8, c * 128 : c * 128 + 128] = fa[slot, n]

    wait_q(A0, lambda i: fa.at[i, pl.ds(0, 1)])
    place((0,))
    send_p(FB, lambda o: frow(0)(p), frow(0))
    wait_q(CR, lambda i: cr.at[i])
    c8(q)[...] = total(cr)
    send_q(CA, lambda o: c8(q), c8)
    wait_q(A1, lambda i: fa.at[i, pl.ds(1, 2)])
    place((1, 2))
    for k in (1, 2, 3):
        send_p(FB + k, lambda o: frow(k)(p), frow(k))
    for c in loads[4:]:
        c.wait()
    wait_p(GN, lambda i: gback.at[i])
    join_columns(gback, lgn_ref)
    for source, turned in ((avg_ref, avg_t), (sq_ref, sq_t)):
        turned[...] = jnp.zeros((K, 128), F32)
        turned[:, :R] = source[...].T

    scale = math.sqrt(D)

    def block(k):
        return slice(k * 128, (k + 1) * 128)

    def cross_shared():
        for k in (1, 2, 3):
            wait_p(FB + k, frow(k))
        wait_q(CA, c8)
        for h in range(2):
            send_p(CB + h, lambda o: crows(h)(p), crows(h))

    def tile_of(k, first, last):
        return fall[k, :, :, first * 128 : last * 128].reshape(128, (last - first) * 128) * unit

    state = {}

    def side_before(k):
        here = block(k)
        a = call[k].reshape(128, K + 128)
        if k:
            a = a - dot3(yf[: k * 128, here], yc[: k * 128, :], ((0,), (0,)))
        yc[here, :] = a

    def side_after(k):
        here = block(k)
        y = dot3(inverse[k], yc[here, :], ((1,), (0,)))
        yc[here, :] = y
        basis_out[:, here] = (y[:, K:] * (scale * root)).T[:R, :]
        rotation = y[:, :K] * (root / scale)
        avg_out[:, here] = dot3(rotation, avg_t[...], ((1,), (0,))).T[:R, :]
        sq_out[:, here] = dot3(rotation * rotation, sq_t[...], ((1,), (0,))).T[:R, :]

    def side(h):
        def run():
            wait_p(CB + h, crows(h))
            side_before(2 * h)
            side_after(2 * h)
            side_before(2 * h + 1)
            if h == 0:
                side_after(1)
        return run

    def wide(k):
        def run():
            if k < 3:
                yf[block(k - 1), (k + 1) * 128 :] = dot(inverse[k - 1], state["a"][:, 128:], ((1,), (0,)), HIGHEST)
                u = yf[: k * 128, block(k)]
                state["a"] = tile_of(k, k + 1, 4) - dot(u, yf[: k * 128, (k + 1) * 128 :], ((0,), (0,)), HIGHEST)
                v = yf[: k * 128, block(k + 1)]
                state["d"] = tile_of(k + 1, k + 1, k + 2) - dot(v, v, ((0,), (0,)), HIGHEST)
        return run

    hooks = {
        (0, 6): cross_shared, (1, 2): wide(1), (2, 2): wide(2),
        (3, 2): side(0), (3, 9): side(1),
    }
    wait_p(FB, frow(0))
    unit = 1.0 / fall[0, 0, 0:1, 0:1]
    root = jnp.sqrt(unit)
    diag[...] = tile_of(0, 0, 1)
    for k in range(4):
        here = block(k)
        out = inverse_factor(
            [diag[8 * i : 8 * i + 8, :] for i in range(16)], {m: f for (j, m), f in hooks.items() if j == k}
        )
        for i in range(16):
            inverse[k, 8 * i : 8 * i + 8, :] = out[i]
        if k < 3:
            if k == 0:
                state["a"], state["d"] = tile_of(0, 1, 4), tile_of(1, 1, 2)
            t = dot(inverse[k], state["a"][:, :128], ((1,), (0,)), HIGHEST)
            yf[here, block(k + 1)] = t
            diag[...] = state["d"] - dot(t, t, ((0,), (0,)), HIGHEST)
    side_after(3)
    for c in started:
        c.wait_send()


def body(grad, left_gram, basis, exp_avg, exp_avg_sq):
    vm = pl.BlockSpec(memory_space=pltpu.VMEM)
    sds = jax.ShapeDtypeStruct
    both = pl.pallas_call(
        kernel,
        out_shape=sds((R, D + 3 * K), F32),
        in_specs=[pl.BlockSpec(memory_space=pltpu.HBM)] * 5,
        out_specs=vm,
        scratch_shapes=[
            pltpu.VMEM((R, D), F32), pltpu.VMEM((R, K), F32), pltpu.VMEM((R, K), F32), pltpu.VMEM((R, K), F32),
            pltpu.VMEM((256, WIDE), BF16), pltpu.VMEM((256, WIDE), BF16),
            pltpu.VMEM((8, R, 256), F32), pltpu.VMEM((8, R, 256), F32),
            pltpu.VMEM((8, R, 256), F32), pltpu.VMEM((8, R, 256), F32),
            pltpu.VMEM((8, R, K), F32), pltpu.VMEM((8, R, K), F32),
            pltpu.VMEM((256, K), F32), pltpu.VMEM((K, 256), F32),
            pltpu.VMEM((8, 3, 8, 128), F32), pltpu.VMEM((8, 3, 8, 128), F32),
            pltpu.VMEM((8, 8, K), F32), pltpu.VMEM((8, 8, K), F32),
            pltpu.VMEM((8, 3, 8, 128), F32),
            pltpu.VMEM((4, 8, 16, K), F32), pltpu.VMEM((4, 8, 16, K + 128), F32),
            pltpu.VMEM((K, K), F32), pltpu.VMEM((K, K + 128), F32),
            pltpu.VMEM((128, 128), F32), pltpu.VMEM((4, 128, 128), F32),
            pltpu.VMEM((K, 128), F32), pltpu.VMEM((K, 128), F32),
            pltpu.SemaphoreType.DMA((20, 8)), pltpu.SemaphoreType.DMA((20, 8)),
            pltpu.SemaphoreType.DMA((2, 14)), pltpu.SemaphoreType.DMA((2, 16)), pltpu.SemaphoreType.DMA((6,)),
        ],
        compiler_params=pltpu.CompilerParams(
            collective_id=0, has_side_effects=True, vmem_limit_bytes=60 * 1024 * 1024
        ),
        cost_estimate=pl.CostEstimate(flops=1_000_000_000, bytes_accessed=2_000_000, transcendentals=0),
        name="soap_refresh",
    )(grad, left_gram, basis, exp_avg, exp_avg_sq)
    return (both[:, :D],) + tuple(both[:, D + i * K : D + i * K + K] for i in range(3))


def solution(mesh):
    placed = P(("layer", "dp"), None)
    return jax.shard_map(
        body, mesh=mesh, in_specs=(placed,) * 5, out_specs=(placed,) * 4, check_vma=False
    )
```

```python
import functools
import math

import jax
import jax.numpy as jnp
from jax import lax
from jax.experimental import pallas as pl
from jax.experimental.pallas import tpu as pltpu
from jax.sharding import PartitionSpec as P

D = 2048
K = 512
R = 32
HIGHEST = lax.Precision.HIGHEST
F32 = jnp.float32
BF16 = jnp.bfloat16
LG, GN, PP, PG, R0, R1, A0, A1, FB, CR, CA, CB = 0, 1, 2, 4, 6, 7, 8, 9, 10, 14, 15, 16
WIDE = D + K


def dot(a, b, dims, precision=None):
    return lax.dot_general(a, b, (dims, ((), ())), precision=precision, preferred_element_type=F32)


def dot3(a, b, dims):
    ah, bh = a.astype(BF16), b.astype(BF16)
    al, bl = (a - ah.astype(F32)).astype(BF16), (b - bh.astype(F32)).astype(BF16)
    return dot(ah, bh, dims) + (dot(ah, bl, dims) + dot(al, bh, dims))


def lane(v, k):
    return jnp.broadcast_to(v[:, k : k + 1], (8, 128))


def sub(v, t):
    return jnp.broadcast_to(v[t : t + 1, :], (8, 128))


def inverse_factor(a_rows, hooks={}):
    row = lax.broadcasted_iota(jnp.int32, (8, 128), 0)
    col = lax.broadcasted_iota(jnp.int32, (8, 128), 1)
    n = len(a_rows)
    a_rows = list(a_rows)
    e_rows = [jnp.where(col == row + 8 * i, 1.0, 0.0).astype(F32) for i in range(n)]
    out = []
    for m in range(n):
        hooks.get(m, lambda: None)()
        r_m, s_m = a_rows[m], e_rows[m]
        c = [lane(r_m, 8 * m + t) for t in range(8)]
        v = jnp.zeros((8, 128), F32)
        for t in range(0, 8, 2):
            first, second, both = row == t, row == t + 1, row // 2 == t // 2
            d00, d10, d11 = sub(c[t], t), sub(c[t], t + 1), sub(c[t + 1], t + 1)
            det = d00 * d11 - d10 * d10
            inv = 1.0 / det
            m0 = jnp.where(first, -1.0, jnp.where(second, 0.0, c[t]))
            m1 = jnp.where(first, 0.0, jnp.where(second, -1.0, c[t + 1]))
            f0, f1 = m0 * d11 - m1 * d10, m1 * d00 - m0 * d10
            s0, s1 = sub(s_m, t), sub(s_m, t + 1)
            root = lax.rsqrt(d00)
            v = jnp.where(first, s0 * root, v)
            v = jnp.where(second, (d00 * s1 - d10 * s0) * (root * lax.rsqrt(det)), v)

            def step(x, x0, x1):
                return jnp.where(both, 0.0, x) - (f0 * x0 + f1 * x1) * inv

            for u in range(t + 2, 8):
                c[u] = step(c[u], sub(c[u], t), sub(c[u], t + 1))
            if m < n - 1:
                r_m = step(r_m, sub(r_m, t), sub(r_m, t + 1))
            if m < n - 1 or t < 6:
                s_m = step(s_m, s0, s1)
        out.append(v)
        if m < n - 1:
            w = [sub(r_m, t) for t in range(8)]
            s = [sub(s_m, t) for t in range(8)]
            for i in range(m + 1, n):
                l = [lane(a_rows[i], 8 * m + t) for t in range(8)]
                for t in range(8):
                    a_rows[i] = a_rows[i] - l[t] * w[t]
                    e_rows[i] = e_rows[i] - l[t] * s[t]
    return out


def split_columns(lg_ref, out_ref):
    low = lax.broadcasted_iota(jnp.int32, (R, 128), 1) < 64
    for x in range(4):
        t = [lg_ref[:, x * 512 + k * 128 : x * 512 + (k + 1) * 128] for k in range(4)]
        for h in range(2):
            a, b = t[2 * h], t[2 * h + 1]
            out_ref[2 * x, :, h * 128 : (h + 1) * 128] = jnp.where(low, a, pltpu.roll(b, 64, 1))
            out_ref[2 * x + 1, :, h * 128 : (h + 1) * 128] = jnp.where(low, pltpu.roll(a, 64, 1), b)


def join_columns(in_ref, out_ref):
    low = lax.broadcasted_iota(jnp.int32, (R, 128), 1) < 64
    for x in range(4):
        for h in range(2):
            a = in_ref[2 * x, :, h * 128 : (h + 1) * 128]
            b = in_ref[2 * x + 1, :, h * 128 : (h + 1) * 128]
            at = x * 512 + h * 256
            out_ref[:, at : at + 128] = jnp.where(low, a, pltpu.roll(b, 64, 1))
            out_ref[:, at + 128 : at + 256] = jnp.where(low, pltpu.roll(a, 64, 1), b)


def kernel(
    grad_hbm, lg_hbm, basis_hbm, avg_hbm, sq_hbm,
    out_ref,
    lg_ref, basis_ref, avg_ref, sq_ref,
    ga, gb, lgs, lgr, gn, gback, pp, pr, pb, pt, fp, fr, cp, cr, fa, fall, call, yf, yc, diag, inverse, avg_t, sq_t,
    send_sem, recv_sem, gather_send, gather_recv, in_sem,
):
    lgn_ref = out_ref.at[:, pl.ds(0, D)]
    basis_out, avg_out, sq_out = [out_ref.at[:, pl.ds(D + i * K, K)] for i in range(3)]
    me = lax.axis_index("dp")
    x, z21, z0, yh = me // 16, (me // 4) % 4, (me // 2) % 2, me % 2
    p = x * 2 + z0
    q = z21 * 2 + yh

    def device(pp_, qq_):
        return {"dp": (pp_ // 2) * 16 + (qq_ // 2) * 4 + (pp_ % 2) * 2 + qq_ % 2}

    def p_peers():
        return [(p + d) % 8 for d in range(1, 8)]

    def q_peers():
        return [(q + d) % 8 for d in range(1, 8)]

    barrier = pltpu.get_barrier_semaphore()
    for o in p_peers():
        pl.semaphore_signal(barrier, inc=1, device_id=device(o, q), device_id_type=pl.DeviceIdType.MESH)
    for o in q_peers():
        pl.semaphore_signal(barrier, inc=1, device_id=device(p, o), device_id_type=pl.DeviceIdType.MESH)

    def rows(ref, i, n=R):
        return ref.at[pl.ds(pl.multiple_of(i * n, n), n)]

    def grad_rows(ref, i):
        return ref.at[pl.ds(pl.multiple_of(i * R, R), R), pl.ds(0, D)]

    def basis_rows(ref, i):
        return ref.at[pl.ds(pl.multiple_of(i * R, R), R), pl.ds(D, K)]

    loads = [
        pltpu.make_async_copy(basis_hbm, basis_ref, in_sem.at[0]),
        pltpu.make_async_copy(grad_hbm, grad_rows(ga, q), in_sem.at[1]),
        pltpu.make_async_copy(grad_hbm, grad_rows(gb, p), in_sem.at[2]),
        pltpu.make_async_copy(lg_hbm, lg_ref, in_sem.at[3]),
        pltpu.make_async_copy(avg_hbm, avg_ref, in_sem.at[4]),
        pltpu.make_async_copy(sq_hbm, sq_ref, in_sem.at[5]),
    ]
    for c in loads:
        c.start()

    def copy(phase, src, dst, to, slot_from, dev):
        return pltpu.make_async_remote_copy(
            src_ref=src, dst_ref=dst,
            send_sem=send_sem.at[phase, to], recv_sem=recv_sem.at[phase, slot_from],
            device_id=dev, device_id_type=pl.DeviceIdType.MESH,
        )

    started = []

    def send_p(phase, src, dst):
        for o in p_peers():
            c = copy(phase, src(o), dst(p), o, p, device(o, q))
            c.start()
            started.append(c)

    def send_q(phase, src, dst):
        for o in q_peers():
            c = copy(phase, src(o), dst(q), o, q, device(p, o))
            c.start()
            started.append(c)

    def wait_p(phase, dst):
        for o in p_peers():
            copy(phase, dst(o), dst(o), o, o, device(o, q)).wait_recv()

    def wait_q(phase, dst):
        for o in q_peers():
            copy(phase, dst(o), dst(o), o, o, device(p, o)).wait_recv()

    loads[0].wait()
    wire = basis_ref[...].astype(BF16)
    basis_rows(ga, q)[...] = wire
    basis_rows(gb, p)[...] = wire
    for c in loads[1:3]:
        c.wait()

    class Group:
        def __init__(self, index, buffer, ring, pair, where):
            self.index, self.buffer, self.ring, self.pair, self.where = index, buffer, ring, pair, where
            self.sent = 0

        def slot(self, step, other):
            pair = (1 - self.pair) if other else self.pair
            return ((self.ring + step) % 4) * 2 + pair

        def half(self, slot, h):
            return rows(self.buffer, slot * 2 + h, 16)

        def copy(self, slot, h, to, n):
            ref = self.half(slot, h)
            return pltpu.make_async_remote_copy(
                src_ref=ref, dst_ref=ref,
                send_sem=gather_send.at[self.index, n], recv_sem=gather_recv.at[self.index, slot * 2 + h],
                device_id=self.where(to), device_id_type=pl.DeviceIdType.MESH,
            )

        def send(self, slot, h, to):
            c = self.copy(slot, h, to, self.sent)
            self.sent += 1
            c.start()
            started.append(c)

        def wait(self, step, other, h):
            slot = self.slot(step, other)
            self.copy(slot, h, self.slot(0, True), 0).wait_recv()
            return slot

        def own(self):
            me_ = self.slot(0, False)
            after, before, partner = self.slot(1, False), self.slot(3, False), self.slot(0, True)
            self.send(me_, 0, partner)
            self.send(me_, 0, after)
            self.send(me_, 1, before)
            self.send(me_, 1, partner)
            self.send(me_, 0, before)
            self.send(me_, 1, after)

        def across(self, h):
            self.send(self.wait(2, False, h), h, self.slot(0, True))

        def relay(self, other):
            self.send(self.wait(3, other, 0), 0, self.slot(1, False))
            self.send(self.wait(1, other, 1), 1, self.slot(3, False))

        def partner(self, h):
            slot = self.wait(0, True, h)
            self.send(slot, h, self.slot(1 + 2 * h, False))
            self.send(slot, h, self.slot(3 - 2 * h, False))

        def rest(self, crossed):
            for other in (False, True):
                self.wait(3, other, 1)
                self.wait(1, other, 0)
                if other and crossed:
                    self.wait(3, other, 0)
                    self.wait(1, other, 1)
                if other or not crossed:
                    self.wait(2, other, 0)
                    self.wait(2, other, 1)

    by_q = Group(0, ga, z21, yh, lambda o: device(p, o))
    by_p = Group(1, gb, x, z0, lambda o: device(o, q))
    pl.semaphore_wait(barrier, 14)
    by_q.own()
    by_p.own()
    by_q.relay(False)
    by_p.partner(0)
    by_p.partner(1)
    loads[3].wait()
    split_columns(lg_ref, lgs)
    lgr[p] = lgs[p]
    send_p(LG, lambda o: lgs.at[o], lambda i: lgr.at[i])
    by_p.relay(False)
    by_q.partner(0)
    by_p.relay(True)
    by_q.across(0)
    by_q.partner(1)
    by_q.across(1)
    by_p.rest(False)
    by_q.rest(True)
    wait_p(LG, lambda i: lgr.at[i])
    gram = dot(gb[:, :D], ga[:, :D], ((1,), (1,)))
    new = 0.95 * lgr[...].reshape(256, 256) + 0.05 * gram
    gn[...] = new.reshape(8, R, 256)
    gback[p] = gn[p]
    high = new.astype(BF16)
    rest = new - high.astype(F32)
    mid = rest.astype(BF16)
    low = (rest - mid.astype(F32)).astype(BF16)
    def total(ref):
        s = ref[0]
        for i in range(1, 8):
            s = s + ref[i]
        return s

    def half(ref, i, h):
        return ref.at[i, :, pl.ds(h * 256, 256)]

    def rows_half(i, h):
        return pb.at[pl.ds(pl.multiple_of(i * R, R), R), pl.ds(h * 256, 256)]

    for h in range(2):
        w = ga[:, D + h * 256 : D + h * 256 + 256]
        part = dot(high, w, ((1,), (0,))) + (dot(mid, w, ((1,), (0,))) + dot(low, w, ((1,), (0,))))
        pp[:, :, h * 256 : h * 256 + 256] = part.reshape(8, R, 256)
        send_p(PP + h, lambda o: half(pp, o, h), lambda i: half(pr, i, h))
    pr[p] = pp[p]
    for h in range(2):
        wait_p(PP + h, lambda i: half(pr, i, h))
        rows_half(p, h)[...] = total(pr.at[:, :, pl.ds(h * 256, 256)])
        send_p(PG + h, lambda o: rows_half(p, h), lambda i: rows_half(i, h))
    own = rows(pb, p)[...]
    call[:, :, :, K:] = jnp.zeros((4, 8, 16, 128), F32)
    own_t = own.T
    for k in range(4):
        for i in range(8):
            at = k * 128 + i * 16
            call[k, i, :, K : K + R] = own_t[at : at + 16]
    for h in range(2):
        wait_p(PG + h, lambda i: rows_half(i, h))
        pt[h * 256 : h * 256 + 256, :] = pb[:, h * 256 : h * 256 + 256].T
    left = jnp.concatenate(
        [pt[pl.ds(pl.multiple_of(k * 128 + p * 16, 16), 16), :] for k in range(4)], axis=0
    )
    part = dot(left, pb[...], ((1,), (0,)), HIGHEST)

    def tiles(slot):
        h, j = slot // 4, slot % 4
        return [(0, h, j), (1, h, j + 1) if j < 3 else (3, h, 3), (2, h, 2 + j % 2)]

    for slot in range(8):
        for n, (k, h, c) in enumerate(tiles(slot)):
            fp[slot, n] = part[k * 16 + h * 8 : k * 16 + h * 8 + 8, c * 128 : c * 128 + 128]
    send_q(R0, lambda o: fp.at[o, pl.ds(0, 1)], lambda i: fr.at[i, pl.ds(0, 1)])
    send_q(R1, lambda o: fp.at[o, pl.ds(1, 2)], lambda i: fr.at[i, pl.ds(1, 2)])
    fr[q] = fp[q]
    cp[...] = dot(left, gb[:, D:].astype(F32), ((1,), (0,)), HIGHEST).reshape(8, 8, K)
    cr[q] = cp[q]

    def frow(k):
        return lambda i: fall.at[k, i, :, pl.ds(k * 128, K - k * 128)]

    def c8(i):
        return call.at[i // 2, p, pl.ds(pl.multiple_of((i % 2) * 8, 8), 8), pl.ds(0, K)]

    def crows(h):
        return lambda i: call.at[pl.ds(2 * h, 2), i, :, pl.ds(0, K)]

    wait_q(R0, lambda i: fr.at[i, pl.ds(0, 1)])
    fa[q, 0] = total(fr.at[:, 0])
    send_q(A0, lambda o: fa.at[q, pl.ds(0, 1)], lambda i: fa.at[i, pl.ds(0, 1)])
    send_q(CR, lambda o: cp.at[o], lambda i: cr.at[i])
    wait_q(R1, lambda i: fr.at[i, pl.ds(1, 2)])
    for n in (1, 2):
        fa[q, n] = total(fr.at[:, n])
    send_q(A1, lambda o: fa.at[q, pl.ds(1, 2)], lambda i: fa.at[i, pl.ds(1, 2)])
    send_p(GN, lambda o: gn.at[o], lambda i: gback.at[i])

    def place(numbers):
        for slot in range(8):
            for n, (k, h, c) in enumerate(tiles(slot)):
                if n in numbers and not (n == 2 and slot % 4 > 1):
                    fall[k, p, h * 8 : h * 8 + 8, c * 128 : c * 128 + 128] = fa[slot, n]

    wait_q(A0, lambda i: fa.at[i, pl.ds(0, 1)])
    place((0,))
    send_p(FB, lambda o: frow(0)(p), frow(0))
    wait_q(CR, lambda i: cr.at[i])
    c8(q)[...] = total(cr)
    send_q(CA, lambda o: c8(q), c8)
    wait_q(A1, lambda i: fa.at[i, pl.ds(1, 2)])
    place((1, 2))
    for k in (1, 2, 3):
        send_p(FB + k, lambda o: frow(k)(p), frow(k))
    for c in loads[4:]:
        c.wait()
    wait_p(GN, lambda i: gback.at[i])
    join_columns(gback, lgn_ref)
    for source, turned in ((avg_ref, avg_t), (sq_ref, sq_t)):
        turned[...] = jnp.zeros((K, 128), F32)
        turned[:, :R] = source[...].T

    scale = math.sqrt(D)

    def block(k):
        return slice(k * 128, (k + 1) * 128)

    def rows_here():
        for k in (1, 2, 3):
            wait_p(FB + k, frow(k))

    def cross_shared():
        wait_q(CA, c8)
        for h in range(2):
            send_p(CB + h, lambda o: crows(h)(p), crows(h))

    def tile_of(k, first, last):
        return fall[k, :, :, first * 128 : last * 128].reshape(128, (last - first) * 128) * unit

    state = {}

    def side_before(k):
        here = block(k)
        a = call[k].reshape(128, K + 128)
        if k:
            a = a - dot3(yf[: k * 128, here], yc[: k * 128, :], ((0,), (0,)))
        yc[here, :] = a

    def side_after(k):
        here = block(k)
        y = dot3(inverse[k], yc[here, :], ((1,), (0,)))
        yc[here, :] = y
        basis_out[:, here] = (y[:, K:] * (scale * root)).T[:R, :]
        rotation = y[:, :K] * (root / scale)
        avg_out[:, here] = dot3(rotation, avg_t[...], ((1,), (0,))).T[:R, :]
        sq_out[:, here] = dot3(rotation * rotation, sq_t[...], ((1,), (0,))).T[:R, :]

    def side(h):
        def run():
            wait_p(CB + h, crows(h))
            side_before(2 * h)
            side_after(2 * h)
            side_before(2 * h + 1)
            if h == 0:
                side_after(1)
        return run

    def wide(k):
        def run():
            if k < 3:
                yf[block(k - 1), (k + 1) * 128 :] = dot(inverse[k - 1], state["a"][:, 128:], ((1,), (0,)), HIGHEST)
                u = yf[: k * 128, block(k)]
                state["a"] = tile_of(k, k + 1, 4) - dot(u, yf[: k * 128, (k + 1) * 128 :], ((0,), (0,)), HIGHEST)
                v = yf[: k * 128, block(k + 1)]
                state["d"] = tile_of(k + 1, k + 1, k + 2) - dot(v, v, ((0,), (0,)), HIGHEST)
        return run

    hooks = {
        (0, 14): rows_here, (1, 3): cross_shared, (1, 2): wide(1), (2, 2): wide(2),
        (3, 2): side(0), (3, 9): side(1),
    }
    wait_p(FB, frow(0))
    unit = 1.0 / fall[0, 0, 0:1, 0:1]
    root = jnp.sqrt(unit)
    diag[...] = tile_of(0, 0, 1)
    for k in range(4):
        here = block(k)
        out = inverse_factor(
            [diag[8 * i : 8 * i + 8, :] for i in range(16)], {m: f for (j, m), f in hooks.items() if j == k}
        )
        for i in range(16):
            inverse[k, 8 * i : 8 * i + 8, :] = out[i]
        if k < 3:
            if k == 0:
                state["a"], state["d"] = tile_of(0, 1, 4), tile_of(1, 1, 2)
            t = dot(inverse[k], state["a"][:, :128], ((1,), (0,)), HIGHEST)
            yf[here, block(k + 1)] = t
            diag[...] = state["d"] - dot(t, t, ((0,), (0,)), HIGHEST)
    side_after(3)
    for c in started:
        c.wait_send()


def body(grad, left_gram, basis, exp_avg, exp_avg_sq):
    vm = pl.BlockSpec(memory_space=pltpu.VMEM)
    sds = jax.ShapeDtypeStruct
    both = pl.pallas_call(
        kernel,
        out_shape=sds((R, D + 3 * K), F32),
        in_specs=[pl.BlockSpec(memory_space=pltpu.HBM)] * 5,
        out_specs=vm,
        scratch_shapes=[
            pltpu.VMEM((R, D), F32), pltpu.VMEM((R, K), F32), pltpu.VMEM((R, K), F32), pltpu.VMEM((R, K), F32),
            pltpu.VMEM((256, WIDE), BF16), pltpu.VMEM((256, WIDE), BF16),
            pltpu.VMEM((8, R, 256), F32), pltpu.VMEM((8, R, 256), F32),
            pltpu.VMEM((8, R, 256), F32), pltpu.VMEM((8, R, 256), F32),
            pltpu.VMEM((8, R, K), F32), pltpu.VMEM((8, R, K), F32),
            pltpu.VMEM((256, K), F32), pltpu.VMEM((K, 256), F32),
            pltpu.VMEM((8, 3, 8, 128), F32), pltpu.VMEM((8, 3, 8, 128), F32),
            pltpu.VMEM((8, 8, K), F32), pltpu.VMEM((8, 8, K), F32),
            pltpu.VMEM((8, 3, 8, 128), F32),
            pltpu.VMEM((4, 8, 16, K), F32), pltpu.VMEM((4, 8, 16, K + 128), F32),
            pltpu.VMEM((K, K), F32), pltpu.VMEM((K, K + 128), F32),
            pltpu.VMEM((128, 128), F32), pltpu.VMEM((4, 128, 128), F32),
            pltpu.VMEM((K, 128), F32), pltpu.VMEM((K, 128), F32),
            pltpu.SemaphoreType.DMA((20, 8)), pltpu.SemaphoreType.DMA((20, 8)),
            pltpu.SemaphoreType.DMA((2, 14)), pltpu.SemaphoreType.DMA((2, 16)), pltpu.SemaphoreType.DMA((6,)),
        ],
        compiler_params=pltpu.CompilerParams(
            collective_id=0, has_side_effects=True, vmem_limit_bytes=60 * 1024 * 1024
        ),
        cost_estimate=pl.CostEstimate(flops=1_000_000_000, bytes_accessed=2_000_000, transcendentals=0),
        name="soap_refresh",
    )(grad, left_gram, basis, exp_avg, exp_avg_sq)
    return (both[:, :D],) + tuple(both[:, D + i * K : D + i * K + K] for i in range(3))


def solution(mesh):
    placed = P(("layer", "dp"), None)
    return jax.shard_map(
        body, mesh=mesh, in_specs=(placed,) * 5, out_specs=(placed,) * 4, check_vma=False
    )
```
